32 devices in a mesh: rep: 4 (over y, x), fsdp: 8 (over z, core).
Axes of the slice: x: 2, y: 2, z: 4, core: 2. Of those that a mesh axis runs over, the one named last changes fastest.
Arguments:
- inputs: bfloat16 [4, 1024, 4096], P('rep', 'fsdp'), may hold values from -6 to 6
- key_grads: bfloat16 [4, 1024, 512], P('rep', 'fsdp'), may hold values from -0.3125 to 0.3125
- weights: float32 [4, 4096, 512], P('rep', 'fsdp'), may hold values from -0.09375 to 0.09375
- first_moment: bfloat16 [4, 4096, 512], P('rep', 'fsdp'), may hold values from -1.25 to 1.25
- second_moment: bfloat16 [4, 4096, 512], P('rep', 'fsdp'), may hold values from 0.099609375 to 1
- drift: float32 [4, 4096, 512], P('rep', 'fsdp'), may hold values from -0.078125 to 0.078125
- momentum: float32 [4096, 512], P(('fsdp', 'rep')), may hold values from -0.0625 to 0.0625
- global_weights: float32 [4096, 512], P(('fsdp', 'rep')), may hold values from -0.09375 to 0.09375
Outputs:
- keys: bfloat16 [4, 1024, 512], P('rep', 'fsdp')
- input_grads: bfloat16 [4, 1024, 4096], P('rep', 'fsdp')
- merged_weights: float32 [4, 4096, 512], P('rep', 'fsdp')
- new_first_moment: bfloat16 [4, 4096, 512], P('rep', 'fsdp')
- new_second_moment: bfloat16 [4, 4096, 512], P('rep', 'fsdp')
- new_momentum: float32 [4096, 512], P(('fsdp', 'rep'))
- new_global: float32 [4096, 512], P(('fsdp', 'rep'))
The draws below stay inside these ranges and needn't reach their ends.
All inputs are finite; a program needn't handle non-finite values.
Results may differ from the reference program's by a relative error of at most 0.02.
Values may be sent and summed in bfloat16 or wider, within the bound.
No kernel may reach another device: no remote copies, remote signals or barrier semaphores. Data moves between devices by JAX's collectives and lax.ppermute only.
A program may use at most 64 MiB of HBM per device.

```python
import math
import jax
import jax.numpy as jnp
from jax import lax

D_WIN = 4096
HEAD = 128
SEQ = 1024
TOK_DEV = 128
KV_COLS = 512
TOK_REP = 1024
N_REP = 4
N_FSDP = 8


def spiked(drawn, key, source, target, blocks, factor):
    owner, partner = [(jnp.arange(drawn.shape[axis_at]) // (drawn.shape[axis_at] // blocks)).reshape([-1 if axis == axis_at else 1 for axis in range(drawn.ndim)]) for axis_at in (source, target)]
    chosen = jax.random.permutation(key, blocks)[partner]
    strong = (owner == chosen) | (owner == (partner + blocks // 2) % blocks)
    return jnp.where(strong, factor * drawn, drawn)


def block_scale(own_key, dims, pieces, least, largest):
    loudness, own = 1.0, jax.random.fold_in(own_key, 6)
    for axis_at, shards_of in pieces:
        draws = jnp.exp(jax.random.uniform(jax.random.fold_in(own, axis_at), (shards_of,), jnp.float32, least / len(pieces), largest / len(pieces)))
        loudness = loudness * jnp.repeat(draws, dims[axis_at] // shards_of).reshape([-1 if axis == axis_at else 1 for axis in range(len(dims))])
    return loudness


def normal_values(own_key, dims, scale, reach, pieces=(), kind=jnp.bfloat16):
    values = jax.random.normal(own_key, dims, jnp.float32) * scale
    if len(pieces) > 0:
        values = block_scale(own_key, dims, pieces, -0.22, 0.18) * values
    return jnp.clip(values, min=-reach, max=reach).astype(kind)


def noise_with(own_key, dims, width, limit, cuts, heavy, kind=jnp.bfloat16):
    values = width * jax.random.normal(own_key, dims, jnp.float32)
    if cuts:
        values = values * block_scale(own_key, dims, cuts, -0.22, 0.18)
    return jnp.clip(spiked(values, jax.random.fold_in(own_key, 3), *heavy), -limit, limit).astype(kind)


def setup_inputs(seed: int = 0) -> dict:
    splits = jax.random.split(jax.random.key(seed), 9)
    return {
        "inputs": normal_values(splits[0], (N_REP, TOK_REP, D_WIN), 1.0, 6.0, ((0, 4), (1, 8))),
        "key_grads": normal_values(splits[1], (N_REP, TOK_REP, KV_COLS), 0.05, 0.3125, ((0, 4), (1, 8))),
        "weights": normal_values(splits[2], (N_REP, D_WIN, KV_COLS), D_WIN ** -0.5, 0.09375, ((0, 4), (1, 8)), jnp.float32),
        "first_moment": normal_values(splits[3], (N_REP, D_WIN, KV_COLS), 0.2, 1.25, ((0, 4), (1, 8))),
        "second_moment": jnp.clip(jnp.exp(math.log(1.0) - 2.306499 * jax.random.uniform(splits[4], (N_REP, D_WIN, KV_COLS), jnp.float32) ** block_scale(splits[4], (N_REP, D_WIN, KV_COLS), ((0, 4), (1, 8)), -0.2, 0.2)), 0.099609375, 1.0).astype(jnp.bfloat16),
        "drift": noise_with(splits[5], (N_REP, D_WIN, KV_COLS), 0.01, 0.078125, ((0, 4), (1, 8)), (0, 1, 4, 2.0), jnp.float32),
        "momentum": normal_values(splits[6], (D_WIN, KV_COLS), 0.01, 0.0625, ((0, 32),), jnp.float32),
        "global_weights": normal_values(splits[7], (D_WIN, KV_COLS), D_WIN ** -0.5, 0.09375, ((0, 32),), jnp.float32),
    }


learning_rate = 0.002
beta_one = 0.9
beta_two = 0.95
adam_epsilon = 1e-08
weight_decay = 0.1
outer_rate = 0.7
outer_beta = 0.9
mixing = 0.5
rope_base = 500000.0

def rope_tables(positions):
    half_size = HEAD // 2
    exponents = jnp.arange(half_size, dtype=jnp.float32) * (2.0 / HEAD)
    inverse_freq = jnp.power(jnp.float32(rope_base), -exponents)
    angles = positions[:, None] * inverse_freq[None, :]
    return (jnp.cos(angles)[:, None, :], jnp.sin(angles)[:, None, :])

def rotate(values, cosine, sines, sign):
    shape = values.shape
    heads = values.reshape(shape[0], shape[1] // HEAD, HEAD)
    half_size = HEAD // 2
    first = heads[..., :half_size]
    second = heads[..., half_size:]
    out_first = first * cosine - sign * second * sines
    out_second = second * cosine + sign * first * sines
    return jnp.concatenate([out_first, out_second], axis=-1).reshape(shape)

def reference(inputs, key_grads, weights, first_moment, second_moment, drift, momentum, global_weights):
    mean_drift = lax.optimization_barrier(jnp.sum(drift, axis=0)) / N_REP
    new_momentum = outer_beta * momentum + mean_drift
    new_global = global_weights - outer_rate * (mean_drift + outer_beta * new_momentum)
    positions = (jnp.arange(TOK_REP) % SEQ).astype(jnp.float32)
    cosine, sines = rope_tables(positions)

    def partial_term(pair):
        return jnp.dot(pair[0].T, pair[1], preferred_element_type=jnp.float32).astype(jnp.bfloat16)

    def one_replica(items):
        tokens, grads, master, first, second = items
        low = master.astype(jnp.bfloat16)
        projected = jnp.dot(tokens, low, preferred_element_type=jnp.float32)
        rotated = rotate(projected, cosine, sines, 1.0).astype(jnp.bfloat16)
        unrotated = rotate(grads.astype(jnp.float32), cosine, sines, -1.0).astype(jnp.bfloat16)
        backward = jnp.dot(unrotated, low.T, preferred_element_type=jnp.float32).astype(jnp.bfloat16)
        token_parts = tokens.reshape(N_FSDP, TOK_DEV, D_WIN)
        grad_parts = unrotated.reshape(N_FSDP, TOK_DEV, KV_COLS)
        partials = lax.map(partial_term, (token_parts, grad_parts))
        gradient = lax.optimization_barrier(jnp.sum(partials.astype(jnp.float32), axis=0))
        moment_one = beta_one * first.astype(jnp.float32) + (1.0 - beta_one) * gradient
        moment_two = beta_two * second.astype(jnp.float32) + (1.0 - beta_two) * gradient * gradient
        stepped = master - learning_rate * (moment_one / (jnp.sqrt(moment_two) + adam_epsilon) + weight_decay * master)
        merged = mixing * stepped + (1.0 - mixing) * new_global
        return (rotated, backward, merged, moment_one.astype(jnp.bfloat16), moment_two.astype(jnp.bfloat16))
    keys, input_grads, merged_weights, first_out, second_out = lax.map(one_replica, (inputs, key_grads, weights, first_moment, second_moment))
    return (keys, input_grads, merged_weights, first_out, second_out, new_momentum, new_global)
```

```python
import functools

import jax
import jax.numpy as jnp
from jax import lax
from jax.experimental import pallas as pl
from jax.experimental.pallas import tpu as pltpu
from jax.sharding import PartitionSpec as P

HEAD = 128
SEQ = 1024

learning_rate = 0.002
beta_one = 0.9
beta_two = 0.95
adam_epsilon = 1e-08
weight_decay = 0.1
outer_rate = 0.7
outer_beta = 0.9
mixing = 0.5
rope_base = 500000.0

VMEM = pl.BlockSpec(memory_space=pltpu.VMEM)
ANY = pl.BlockSpec(memory_space=pl.ANY)
PARAMS = pltpu.CompilerParams(vmem_limit_bytes=10 * 1024 * 1024)
F32 = jnp.float32
BF16 = jnp.bfloat16


def array(shape, kind):
    return jax.ShapeDtypeStruct(shape, kind)


def cost(flops, bytes_accessed):
    return pl.CostEstimate(
        flops=10 * flops, bytes_accessed=10 * bytes_accessed, transcendentals=0
    )


def position(line):
    shard = lax.axis_index("fsdp")
    place, core = lax.div(shard, 2), lax.rem(shard, 2)
    ahead = 1 - 2 * core
    behind = jnp.where(core == 0, place, line - 1 - place)
    return place, core, ahead, behind


def block_at(place, parity, rows):
    return pl.multiple_of((2 * place + parity) * rows, 128)


def rotate_block(values, cosine, sines):
    heads = []
    for at in range(0, values.shape[1], HEAD):
        head = values[:, at : at + HEAD]
        heads.append(head * cosine + pltpu.roll(head, HEAD // 2, 1) * sines)
    return jnp.concatenate(heads, axis=1)


def rope_tables(shard, tokens):
    half_size = HEAD // 2
    token = lax.broadcasted_iota(jnp.int32, (tokens, HEAD), 0)
    column = lax.broadcasted_iota(jnp.int32, (tokens, HEAD), 1)
    exponents = lax.rem(column, half_size).astype(F32) * (2.0 / HEAD)
    inverse_freq = jnp.power(F32(rope_base), -exponents)
    angles = lax.rem(shard * tokens + token, SEQ).astype(F32) * inverse_freq
    sines = jnp.sin(angles)
    return jnp.cos(angles), jnp.where(column < half_size, -sines, sines)


def round_kernel(weights, low, held, sems):
    parts = sems.shape[0]
    size = weights.shape[0] // parts

    def copy(i):
        at = pl.ds(i * size, size)
        return pltpu.make_async_copy(weights.at[at, :], held.at[at, :], sems.at[i])

    for i in range(parts):
        copy(i).start()
    for i in range(parts):
        copy(i).wait()
        low[i * size : (i + 1) * size, :] = held[i * size : (i + 1) * size, :].astype(BF16)


def tables_kernel(line, tokens, cosine, sines):
    place, core, _, _ = position(line)
    for half in range(2):
        at = pl.ds(half * tokens, tokens)
        shard = 2 * place + jnp.bitwise_xor(core, half)
        cosine[at, :], sines[at, :] = rope_tables(shard, tokens)


def gradient_term(x, xp, unrotated, at, size):
    columns = pl.ds(at, size)
    left = jnp.concatenate([x[:, columns], xp[:, columns]], axis=0)
    return lax.dot_general(
        left, unrotated[...], (((0,), (0,)), ((), ())), preferred_element_type=F32
    )


def project(x, xp, unrotated, piece, total, stage, other, at, grads, sem):
    columns = pl.ds(at, piece.shape[0])
    tokens = x.shape[0]
    both = jnp.concatenate([x[:, columns], xp[:, columns]], axis=0)
    total[...] += jnp.dot(both, piece[...], preferred_element_type=F32)
    made = lax.dot_general(
        unrotated[...], piece[...], (((1,), (1,)), ((), ())), preferred_element_type=F32
    ).astype(BF16)
    stage[...] = made[:tokens, :]
    other[...] = made[tokens:, :]
    pltpu.make_async_copy(stage, grads.at[:, columns], sem).start()


def project_wait(stage, grads, at, sem):
    pltpu.make_async_copy(stage, grads.at[:, pl.ds(at, stage.shape[1])], sem).wait()


def local_kernel(line, x, xp, kg, kgp, low, cosine, sines, *refs):
    unrotated, total, other, grads, stage, sem = refs
    tokens = x.shape[0]
    place, core, _, _ = position(line)
    for half, source in enumerate((kg, kgp)):
        at = pl.ds(half * tokens, tokens)
        unrotated[at, :] = rotate_block(
            source[...].astype(F32), cosine[at, :], -sines[at, :]
        ).astype(BF16)
    total[...] = jnp.zeros_like(total)
    at = block_at(place, core, low.shape[0])
    project(x, xp, unrotated, low, total, stage, other, at, grads, sem)
    project_wait(stage, grads, at, sem)


def project_kernel(line, hop, x, xp, unrotated, total_in, grads_in, *refs):
    del grads_in
    first, second, total, other, grads, stage, sems = refs
    tokens = x.shape[0]
    rows = first.shape[0]
    place, core, ahead, behind = position(line)
    total[...] = total_in[...]

    @pl.when(behind >= hop)
    def _():
        work = [(first, core), (second, 1 - core)]
        ats = [block_at(place - hop * ahead, parity, rows) for _, parity in work]
        for i, (piece, _) in enumerate(work):
            into = other.at[:, i * rows : (i + 1) * rows]
            project(
                x, xp, unrotated, piece, total, stage.at[i], into, ats[i], grads, sems.at[i]
            )
        for i in range(2):
            project_wait(stage.at[i], grads, ats[i], sems.at[i])

    if hop == line - 1:
        other[:, 2 * rows :] = total[tokens:, :].astype(BF16)


def merge_kernel(line, cosine, sines, total, grads_in, *refs):
    del grads_in
    others = refs[:line]
    keys, grads, partial, sems, sem = refs[line:]
    tokens, _ = keys.shape
    rows = others[0].shape[1]
    place, core, ahead, behind = position(line)
    work = [(behind >= 0, place, 1 - core, others[0].at[:, :])]
    for hop in range(1, line):
        for i, parity in enumerate((1 - core, core)):
            part = others[hop].at[:, i * rows : (i + 1) * rows]
            work.append((behind + hop < line, place + hop * ahead, parity, part))

    def copy(i):
        _, owner, parity, part = work[i]
        at = pl.ds(block_at(owner, parity, rows), rows)
        return pltpu.make_async_copy(part, grads.at[:, at], sems.at[i])

    rest = pltpu.make_async_copy(others[line - 1].at[:, 2 * rows :], partial, sem)
    rest.start()
    for i in range(len(work)):
        pl.when(work[i][0])(lambda i=i: copy(i).start())
    rest.wait()
    keys[...] = rotate_block(
        total[:tokens, :] + partial[...].astype(F32), cosine[:tokens, :], sines[:tokens, :]
    ).astype(BF16)
    for i in range(len(work)):
        pl.when(work[i][0])(lambda i=i: copy(i).wait())


def step_kernel(line, slot, half, arrived, x, xp, unrotated, sent):
    place, core, ahead, behind = position(line)
    rows = arrived.shape[0]
    size = min(rows, 256)
    parity = core if half else 1 - core

    @pl.when(behind >= slot)
    def _():
        sent[...] = arrived[...]

    @pl.when(behind < slot)
    def _():
        owner = place + (line - slot) * ahead
        for at in range(0, rows, size):
            term = gradient_term(
                x, xp, unrotated, pl.multiple_of(block_at(owner, parity, rows) + at, 128), size
            )
            sent[at : at + size, :] = (arrived[at : at + size, :].astype(F32) + term).astype(BF16)


def early_kernel(line, x, xp, unrotated, swapped, summed):
    place, core, _, _ = position(line)
    rows = swapped.shape[0]
    size = min(rows, 256)
    for at in range(0, rows, size):
        term = gradient_term(
            x, xp, unrotated, pl.multiple_of(block_at(place, core, rows) + at, 128), size
        )
        summed[at : at + size, :] = swapped[at : at + size, :].astype(F32) + term


def update_kernel(summed, arrived, first, second, base, merged, first_out, second_out, *scratch):
    merged_v, first_v, second_v, sem = scratch
    rows = summed.shape[0]
    parts = 4
    size = rows // parts
    chunk = min(size, 32)
    outs = ((merged_v, merged), (first_v, first_out), (second_v, second_out))

    def copies(part):
        at = pl.ds(part * size, size)
        return [
            pltpu.make_async_copy(source.at[at, :], target.at[at, :], sem.at[part, i])
            for i, (source, target) in enumerate(outs)
        ]

    for part in range(parts):

        def some(i, carry, part=part):
            at = pl.ds(pl.multiple_of(part * size + i * chunk, 16), chunk)
            gradient = summed[at, :] + arrived[at, :].astype(F32)
            one = beta_one * first[at, :].astype(F32) + (1.0 - beta_one) * gradient
            two = beta_two * second[at, :].astype(F32) + (1.0 - beta_two) * gradient * gradient
            step = one / (jnp.sqrt(two) + adam_epsilon)
            merged_v[at, :] = base[at, :] - (mixing * learning_rate) * step
            first_v[at, :] = one.astype(BF16)
            second_v[at, :] = two.astype(BF16)
            return carry

        lax.fori_loop(0, size // chunk, some, 0, unroll=True)
        for copy in copies(part):
            copy.start()
    for part in range(parts):
        for copy in copies(part):
            copy.wait()


outer_held = outer_rate * outer_beta * outer_beta
outer_slope = outer_rate * (1.0 + outer_beta)


def pack_kernel(drift, momentum, global_weights, packed):
    rows = drift.shape[0]
    packed[:rows, :] = drift[...].astype(BF16)
    packed[rows:, :] = (global_weights[...] - outer_held * momentum[...]).astype(BF16)


def repack_kernel(drift, mine, other, packed):
    rows = drift.shape[0]
    size = mine.shape[0] - rows
    packed[:rows, :] = (drift[...] + other[:rows, :].astype(F32)).astype(BF16)
    packed[rows : rows + size, :] = mine[rows:, :]
    packed[rows + size :, :] = other[rows:, :]


def outer_kernel(drift, near, far, momentum, global_weights, weights, *refs):
    base, new_momentum, new_global = refs
    rows = drift.shape[0]
    size = momentum.shape[0]
    replica = lax.axis_index("rep")
    core = lax.rem(lax.axis_index("fsdp"), 2)
    held = (None, near.at[rows:, :], far.at[rows : rows + size, :], far.at[rows + size :, :])
    for shift, other in enumerate((0, 1 + core, 2 - core, 3)):
        at = pl.ds(pl.multiple_of(jnp.bitwise_xor(replica, other) * size, size), size)
        total = drift[at, :] + near[at, :].astype(F32) + far[at, :].astype(F32)
        mean_drift = total / 4
        if shift == 0:
            moment = outer_beta * momentum[...] + mean_drift
            updated = global_weights[...] - outer_rate * (mean_drift + outer_beta * moment)
            new_momentum[...] = moment
            new_global[...] = updated
        else:
            updated = held[shift][...].astype(F32) - outer_slope * mean_drift
        base[at, :] = (mixing * (1.0 - learning_rate * weight_decay)) * weights[at, :] + (
            1.0 - mixing
        ) * updated


def pairs_of(turn, shards):
    return [
        (i * shards + j, (i ^ (1 + (j + turn) % 2)) * shards + j)
        for i in range(4)
        for j in range(shards)
    ]


def outer_pack(drift, momentum, global_weights):
    rows, columns = drift.shape
    packed = pl.pallas_call(
        pack_kernel,
        out_shape=array((rows + momentum.shape[0], columns), BF16),
        in_specs=[VMEM] * 3,
        out_specs=VMEM,
        compiler_params=PARAMS,
        cost_estimate=cost(0, 0),
        name="pack",
    )(drift, momentum, global_weights)
    near = lax.ppermute(packed, ("rep", "fsdp"), pairs_of(0, lax.axis_size("fsdp")))
    return packed, near


def outer_repack(drift, packed, near):
    rows, columns = drift.shape
    repacked = pl.pallas_call(
        repack_kernel,
        out_shape=array((2 * packed.shape[0] - rows, columns), BF16),
        in_specs=[VMEM] * 3,
        out_specs=VMEM,
        compiler_params=PARAMS,
        cost_estimate=cost(0, 0),
        name="repack",
    )(drift, packed, near)
    return repacked, lax.ppermute(repacked, ("rep", "fsdp"), pairs_of(1, lax.axis_size("fsdp")))


def outer_end(drift, near, far, momentum, global_weights, weights):
    rows, columns = drift.shape
    size = momentum.shape[0]
    return pl.pallas_call(
        outer_kernel,
        out_shape=(
            array((rows, columns), F32),
            array((size, columns), F32),
            array((size, columns), F32),
        ),
        in_specs=[VMEM] * 6,
        out_specs=(VMEM,) * 3,
        compiler_params=PARAMS,
        cost_estimate=cost(0, 0),
        name="outer",
    )(drift, near, far, momentum, global_weights, weights)


def outer_plain(drift, momentum, global_weights, weights):
    replicas = lax.axis_size("rep")
    size = momentum.shape[0]
    mean_drift = lax.psum(drift, "rep") / replicas
    whole = [lax.all_gather(a, "rep", axis=0, tiled=True) for a in (momentum, global_weights)]
    moment = outer_beta * whole[0] + mean_drift
    updated = whole[1] - outer_rate * (mean_drift + outer_beta * moment)
    base = (mixing * (1.0 - learning_rate * weight_decay)) * weights + (1.0 - mixing) * updated
    at = lax.axis_index("rep") * size
    return (
        base,
        lax.dynamic_slice_in_dim(moment, at, size, 0),
        lax.dynamic_slice_in_dim(updated, at, size, 0),
    )


def after(first, then):
    return lax.optimization_barrier((first, then))[0]


def body(inputs, key_grads, weights, first_moment, second_moment, drift, momentum, global_weights):
    x, kg, master = inputs[0], key_grads[0], weights[0]
    tokens, depth = x.shape
    rows, columns = master.shape
    shards = lax.axis_size("fsdp")
    line = shards // 2
    swap = [(i, i ^ 1) for i in range(shards)]
    onward = [(i, i + 2) for i in range(0, shards - 2, 2)]
    onward += [(i, i - 2) for i in range(3, shards, 2)]
    across = [(i, j ^ 1) for i, j in onward]
    behind = [(i ^ 1, j) for i, j in onward]
    piece = array((rows, columns), BF16)
    cells = rows * columns
    summed_cost = cost(4 * tokens * cells, 6 * cells + 4 * tokens * rows)

    parts = min(8, rows // 16)
    low = pl.pallas_call(
        round_kernel,
        out_shape=piece,
        in_specs=[pl.BlockSpec(memory_space=pltpu.HBM)],
        out_specs=VMEM,
        scratch_shapes=[pltpu.VMEM((rows, columns), F32), pltpu.SemaphoreType.DMA((parts,))],
        compiler_params=PARAMS,
        cost_estimate=cost(0, 0),
        name="round",
    )(master)
    first_a = lax.ppermute(low, "fsdp", onward)
    cosine, sines = pl.pallas_call(
        functools.partial(tables_kernel, line, tokens),
        out_shape=(array((2 * tokens, HEAD), F32),) * 2,
        out_specs=(VMEM, VMEM),
        compiler_params=PARAMS,
        cost_estimate=cost(0, 0),
        name="tables",
    )()
    xp = lax.ppermute(after(x, low), "fsdp", swap)
    kgp = lax.ppermute(after(kg, low), "fsdp", swap)

    unrotated, total, other, input_grads = pl.pallas_call(
        functools.partial(local_kernel, line),
        out_shape=(
            array((2 * tokens, columns), BF16),
            array((2 * tokens, columns), F32),
            array((tokens, rows), BF16),
            array((tokens, depth), BF16),
        ),
        in_specs=[VMEM] * 7,
        out_specs=(VMEM,) * 3 + (ANY,),
        scratch_shapes=[pltpu.VMEM((tokens, rows), BF16), pltpu.SemaphoreType.DMA],
        compiler_params=PARAMS,
        cost_estimate=cost(0, 0),
        name="local",
    )(x, xp, kg, kgp, low, cosine, sines)

    first_b = lax.ppermute(after(low, unrotated), "fsdp", behind)
    arrived = {1: (first_a, first_b)}

    def step(slot, half, value):
        return pl.pallas_call(
            functools.partial(step_kernel, line, slot, half),
            out_shape=piece,
            in_specs=[VMEM] * 4,
            out_specs=VMEM,
            compiler_params=PARAMS,
            cost_estimate=summed_cost,
            name=f"step{slot}{'ab'[half]}",
        )(value, x, xp, unrotated)

    others = [lax.ppermute(other, "fsdp", swap)]

    def project_hop(hop, pieces, total, input_grads):
        wide = 2 * rows + (columns if hop == line - 1 else 0)
        return pl.pallas_call(
            functools.partial(project_kernel, line, hop),
            out_shape=(
                array((2 * tokens, columns), F32),
                array((tokens, wide), BF16),
                array((tokens, depth), BF16),
            ),
            in_specs=[VMEM] * 4 + [ANY] + [VMEM] * 2,
            out_specs=(VMEM, VMEM, ANY),
            scratch_shapes=[
                pltpu.VMEM((2, tokens, rows), BF16),
                pltpu.SemaphoreType.DMA((2,)),
            ],
            input_output_aliases={4: 2},
            compiler_params=PARAMS,
            cost_estimate=cost(16 * tokens * cells, 8 * cells),
            name=f"project{hop}",
        )(x, xp, unrotated, total, input_grads, *pieces)

    pairwise = lax.axis_size("rep") == 4
    delta = drift[0]
    if not pairwise:
        base, new_momentum, new_global = outer_plain(delta, momentum, global_weights, master)
    for slot in range(1, line):
        value = arrived[slot][0]
        if slot > 1:
            value = after(value, sent)
        sent = step(slot, 0, value)
        first = lax.ppermute(sent, "fsdp", across if slot == line - 1 else onward)
        value = arrived[slot][1]
        if pairwise and slot == 1:
            packed, near = outer_pack(after(delta, sent), momentum, global_weights)
        if pairwise and slot == 2:
            repacked, far = outer_repack(after(delta, sent), packed, near)
        if pairwise and slot == 3:
            base, new_momentum, new_global = outer_end(
                after(delta, sent), near, far, momentum, global_weights, master
            )
        sent = step(slot, 1, after(value, sent))
        arrived[slot + 1] = (first, lax.ppermute(sent, "fsdp", onward))
        total, other, input_grads = project_hop(
            slot, arrived[slot], after(total, sent), input_grads
        )
        others.append(lax.ppermute(other, "fsdp", swap))
    sum_swapped, sum_own = arrived[line]

    summed = pl.pallas_call(
        functools.partial(early_kernel, line),
        out_shape=array((rows, columns), F32),
        in_specs=[VMEM] * 4,
        out_specs=VMEM,
        compiler_params=PARAMS,
        cost_estimate=cost(0, 0),
        name="early",
    )(x, xp, unrotated, sum_swapped)
    work = 2 * line - 1
    keys, input_grads = pl.pallas_call(
        functools.partial(merge_kernel, line),
        out_shape=(array((tokens, columns), BF16), array((tokens, depth), BF16)),
        in_specs=[VMEM] * 3 + [ANY] * (1 + line),
        out_specs=(VMEM, ANY),
        scratch_shapes=[
            pltpu.VMEM((tokens, columns), BF16),
            pltpu.SemaphoreType.DMA((work,)),
            pltpu.SemaphoreType.DMA,
        ],
        input_output_aliases={3: 1},
        compiler_params=PARAMS,
        cost_estimate=cost(0, 0),
        name="merge",
    )(cosine, sines, after(total, summed), input_grads, *others)
    sum_own = after(sum_own, keys)
    merged, first_out, second_out = pl.pallas_call(
        update_kernel,
        out_shape=(
            array((rows, columns), F32),
            array((rows, columns), BF16),
            array((rows, columns), BF16),
        ),
        in_specs=[VMEM] * 5,
        out_specs=(ANY,) * 3,
        scratch_shapes=[
            pltpu.VMEM((rows, columns), F32),
            pltpu.VMEM((rows, columns), BF16),
            pltpu.VMEM((rows, columns), BF16),
            pltpu.SemaphoreType.DMA((4, 3)),
        ],
        compiler_params=PARAMS,
        cost_estimate=cost(20 * cells, 18 * cells),
        name="update",
    )(summed, sum_own, first_moment[0], second_moment[0], base)
    return (
        keys[None],
        input_grads[None],
        merged[None],
        first_out[None],
        second_out[None],
        new_momentum,
        new_global,
    )


def solution(mesh):
    sharded = P("rep", "fsdp", None)
    rows = P(("fsdp", "rep"), None)
    return jax.shard_map(
        body,
        mesh=mesh,
        in_specs=(sharded,) * 6 + (rows,) * 2,
        out_specs=(sharded,) * 5 + (rows,) * 2,
        check_vma=False,
    )
```

```python
import functools

import jax
import jax.numpy as jnp
from jax import lax
from jax.experimental import pallas as pl
from jax.experimental.pallas import tpu as pltpu
from jax.sharding import PartitionSpec as P

HEAD = 128
SEQ = 1024

learning_rate = 0.002
beta_one = 0.9
beta_two = 0.95
adam_epsilon = 1e-08
weight_decay = 0.1
outer_rate = 0.7
outer_beta = 0.9
mixing = 0.5
rope_base = 500000.0

VMEM = pl.BlockSpec(memory_space=pltpu.VMEM)
ANY = pl.BlockSpec(memory_space=pl.ANY)
PARAMS = pltpu.CompilerParams(vmem_limit_bytes=10 * 1024 * 1024)
F32 = jnp.float32
BF16 = jnp.bfloat16


def array(shape, kind):
    return jax.ShapeDtypeStruct(shape, kind)


def cost(flops, bytes_accessed):
    return pl.CostEstimate(
        flops=10 * flops, bytes_accessed=10 * bytes_accessed, transcendentals=0
    )


def position(line):
    shard = lax.axis_index("fsdp")
    place, core = lax.div(shard, 2), lax.rem(shard, 2)
    ahead = 1 - 2 * core
    behind = jnp.where(core == 0, place, line - 1 - place)
    return place, core, ahead, behind


def block_at(place, parity, rows):
    return pl.multiple_of((2 * place + parity) * rows, 128)


def rotate_block(values, cosine, sines):
    heads = []
    for at in range(0, values.shape[1], HEAD):
        head = values[:, at : at + HEAD]
        heads.append(head * cosine + pltpu.roll(head, HEAD // 2, 1) * sines)
    return jnp.concatenate(heads, axis=1)


def rope_tables(shard, tokens):
    half_size = HEAD // 2
    token = lax.broadcasted_iota(jnp.int32, (tokens, HEAD), 0)
    column = lax.broadcasted_iota(jnp.int32, (tokens, HEAD), 1)
    exponents = lax.rem(column, half_size).astype(F32) * (2.0 / HEAD)
    inverse_freq = jnp.power(F32(rope_base), -exponents)
    angles = lax.rem(shard * tokens + token, SEQ).astype(F32) * inverse_freq
    sines = jnp.sin(angles)
    return jnp.cos(angles), jnp.where(column < half_size, -sines, sines)


def gradient_term(x, xp, unrotated, at, size):
    columns = pl.ds(at, size)
    left = jnp.concatenate([x[:, columns], xp[:, columns]], axis=0)
    return lax.dot_general(
        left, unrotated[...], (((0,), (0,)), ((), ())), preferred_element_type=F32
    )


def project(x, xp, unrotated, piece, total, stage, other, at, grads, sem):
    columns = pl.ds(at, piece.shape[0])
    tokens = x.shape[0]
    both = jnp.concatenate([x[:, columns], xp[:, columns]], axis=0)
    total[...] += jnp.dot(both, piece[...], preferred_element_type=F32)
    made = lax.dot_general(
        unrotated[...], piece[...], (((1,), (1,)), ((), ())), preferred_element_type=F32
    ).astype(BF16)
    stage[...] = made[:tokens, :]
    other[...] = made[tokens:, :]
    pltpu.make_async_copy(stage, grads.at[:, columns], sem).start()


def project_wait(stage, grads, at, sem):
    pltpu.make_async_copy(stage, grads.at[:, pl.ds(at, stage.shape[1])], sem).wait()


def local_kernel(line, x, xp, kg, kgp, low, *refs):
    unrotated, cosine, sines, total, other, grads, stage, sem = refs
    tokens = x.shape[0]
    place, core, _, _ = position(line)
    shard = 2 * place + core
    for half, source in enumerate((kg, kgp)):
        cosines, signed = rope_tables(jnp.bitwise_xor(shard, half), tokens)
        unrotated[half * tokens : (half + 1) * tokens, :] = rotate_block(
            source[...].astype(F32), cosines, -signed
        ).astype(BF16)
        if half == 0:
            cosine[...] = cosines
            sines[...] = signed
    total[...] = jnp.zeros_like(total)
    at = block_at(place, core, low.shape[0])
    project(x, xp, unrotated, low, total, stage, other, at, grads, sem)
    project_wait(stage, grads, at, sem)


def project_kernel(line, hop, x, xp, unrotated, total_in, grads_in, *refs):
    del grads_in
    first, second, total, other, grads, stage, sems = refs
    tokens = x.shape[0]
    rows = first.shape[0]
    place, core, ahead, behind = position(line)
    total[...] = total_in[...]

    @pl.when(behind >= hop)
    def _():
        work = [(first, core), (second, 1 - core)]
        ats = [block_at(place - hop * ahead, parity, rows) for _, parity in work]
        for i, (piece, _) in enumerate(work):
            into = other.at[:, i * rows : (i + 1) * rows]
            project(
                x, xp, unrotated, piece, total, stage.at[i], into, ats[i], grads, sems.at[i]
            )
        for i in range(2):
            project_wait(stage.at[i], grads, ats[i], sems.at[i])

    if hop == line - 1:
        other[:, 2 * rows :] = total[tokens:, :].astype(BF16)


def merge_kernel(line, cosine, sines, total, grads_in, *refs):
    del grads_in
    others = refs[:line]
    keys, grads, partial, sems, sem = refs[line:]
    tokens, _ = keys.shape
    rows = others[0].shape[1]
    place, core, ahead, behind = position(line)
    work = [(behind >= 0, place, 1 - core, others[0].at[:, :])]
    for hop in range(1, line):
        for i, parity in enumerate((1 - core, core)):
            part = others[hop].at[:, i * rows : (i + 1) * rows]
            work.append((behind + hop < line, place + hop * ahead, parity, part))

    def copy(i):
        _, owner, parity, part = work[i]
        at = pl.ds(block_at(owner, parity, rows), rows)
        return pltpu.make_async_copy(part, grads.at[:, at], sems.at[i])

    rest = pltpu.make_async_copy(others[line - 1].at[:, 2 * rows :], partial, sem)
    rest.start()
    for i in range(len(work)):
        pl.when(work[i][0])(lambda i=i: copy(i).start())
    rest.wait()
    keys[...] = rotate_block(
        total[:tokens, :] + partial[...].astype(F32), cosine[...], sines[...]
    ).astype(BF16)
    for i in range(len(work)):
        pl.when(work[i][0])(lambda i=i: copy(i).wait())


def step_kernel(line, slot, half, arrived, x, xp, unrotated, sent):
    place, core, ahead, behind = position(line)
    rows = arrived.shape[0]
    size = min(rows, 256)
    parity = core if half else 1 - core

    @pl.when(behind >= slot)
    def _():
        sent[...] = arrived[...]

    @pl.when(behind < slot)
    def _():
        owner = place + (line - slot) * ahead
        for at in range(0, rows, size):
            term = gradient_term(
                x, xp, unrotated, pl.multiple_of(block_at(owner, parity, rows) + at, 128), size
            )
            before = arrived[at : at + size, :].astype(F32)
            sent[at : at + size, :] = (term + jnp.where(behind > 0, before, 0.0)).astype(BF16)


def early_kernel(line, x, xp, unrotated, swapped, summed):
    place, core, _, behind = position(line)
    rows = swapped.shape[0]
    size = min(rows, 256)
    for at in range(0, rows, size):
        term = gradient_term(
            x, xp, unrotated, pl.multiple_of(block_at(place, core, rows) + at, 128), size
        )
        other = swapped[at : at + size, :].astype(F32)
        summed[at : at + size, :] = term + jnp.where(behind < line - 1, other, 0.0)


def update_kernel(line, summed, arrived, first, second, base, merged, first_out, second_out, *scratch):
    merged_v, first_v, second_v, sem = scratch
    behind = position(line)[3]
    rows = summed.shape[0]
    parts = 4
    size = rows // parts
    chunk = min(size, 32)
    outs = ((merged_v, merged), (first_v, first_out), (second_v, second_out))

    def copies(part):
        at = pl.ds(part * size, size)
        return [
            pltpu.make_async_copy(source.at[at, :], target.at[at, :], sem.at[part, i])
            for i, (source, target) in enumerate(outs)
        ]

    for part in range(parts):

        def some(i, carry, part=part):
            at = pl.ds(pl.multiple_of(part * size + i * chunk, 16), chunk)
            gradient = summed[at, :] + jnp.where(behind > 0, arrived[at, :].astype(F32), 0.0)
            one = beta_one * first[at, :].astype(F32) + (1.0 - beta_one) * gradient
            two = beta_two * second[at, :].astype(F32) + (1.0 - beta_two) * gradient * gradient
            inverse = lax.rsqrt(two)
            step = one * (inverse * (2.0 - (two * inverse + adam_epsilon) * inverse))
            merged_v[at, :] = base[at, :] - (mixing * learning_rate) * step
            first_v[at, :] = one.astype(BF16)
            second_v[at, :] = two.astype(BF16)
            return carry

        lax.fori_loop(0, size // chunk, some, 0, unroll=True)
        for copy in copies(part):
            copy.start()
    for part in range(parts):
        for copy in copies(part):
            copy.wait()


outer_held = outer_rate * outer_beta * outer_beta
outer_slope = outer_rate * (1.0 + outer_beta)


def pack_kernel(drift, momentum, global_weights, packed):
    rows = drift.shape[0]
    packed[:rows, :] = drift[...].astype(BF16)
    packed[rows:, :] = (global_weights[...] - outer_held * momentum[...]).astype(BF16)


def repack_kernel(drift, mine, other, packed):
    rows = drift.shape[0]
    size = mine.shape[0] - rows
    packed[:rows, :] = (drift[...] + other[:rows, :].astype(F32)).astype(BF16)
    packed[rows : rows + size, :] = mine[rows:, :]
    packed[rows + size :, :] = other[rows:, :]


def outer_kernel(drift, near, far, momentum, global_weights, weights, *refs):
    base, new_momentum, new_global = refs
    rows = drift.shape[0]
    size = momentum.shape[0]
    replica = lax.axis_index("rep")
    core = lax.rem(lax.axis_index("fsdp"), 2)
    held = (None, near.at[rows:, :], far.at[rows : rows + size, :], far.at[rows + size :, :])
    for shift, other in enumerate((0, 1 + core, 2 - core, 3)):
        at = pl.ds(pl.multiple_of(jnp.bitwise_xor(replica, other) * size, size), size)
        total = drift[at, :] + near[at, :].astype(F32) + far[at, :].astype(F32)
        mean_drift = total / 4
        if shift == 0:
            moment = outer_beta * momentum[...] + mean_drift
            updated = global_weights[...] - outer_rate * (mean_drift + outer_beta * moment)
            new_momentum[...] = moment
            new_global[...] = updated
        else:
            updated = held[shift][...].astype(F32) - outer_slope * mean_drift
        base[at, :] = (mixing * (1.0 - learning_rate * weight_decay)) * weights[at, :] + (
            1.0 - mixing
        ) * updated


def pairs_of(turn, shards):
    return [
        (i * shards + j, (i ^ (1 + (j + turn) % 2)) * shards + j)
        for i in range(4)
        for j in range(shards)
    ]


def outer_pack(drift, momentum, global_weights):
    rows, columns = drift.shape
    packed = pl.pallas_call(
        pack_kernel,
        out_shape=array((rows + momentum.shape[0], columns), BF16),
        in_specs=[VMEM] * 3,
        out_specs=VMEM,
        compiler_params=PARAMS,
        cost_estimate=cost(0, 0),
        name="pack",
    )(drift, momentum, global_weights)
    near = lax.ppermute(packed, ("rep", "fsdp"), pairs_of(0, lax.axis_size("fsdp")))
    return packed, near


def outer_repack(drift, packed, near):
    rows, columns = drift.shape
    repacked = pl.pallas_call(
        repack_kernel,
        out_shape=array((2 * packed.shape[0] - rows, columns), BF16),
        in_specs=[VMEM] * 3,
        out_specs=VMEM,
        compiler_params=PARAMS,
        cost_estimate=cost(0, 0),
        name="repack",
    )(drift, packed, near)
    return repacked, lax.ppermute(repacked, ("rep", "fsdp"), pairs_of(1, lax.axis_size("fsdp")))


def outer_end(drift, near, far, momentum, global_weights, weights):
    rows, columns = drift.shape
    size = momentum.shape[0]
    return pl.pallas_call(
        outer_kernel,
        out_shape=(
            array((rows, columns), F32),
            array((size, columns), F32),
            array((size, columns), F32),
        ),
        in_specs=[VMEM] * 6,
        out_specs=(VMEM,) * 3,
        compiler_params=PARAMS,
        cost_estimate=cost(0, 0),
        name="outer",
    )(drift, near, far, momentum, global_weights, weights)


def outer_plain(drift, momentum, global_weights, weights):
    replicas = lax.axis_size("rep")
    size = momentum.shape[0]
    mean_drift = lax.psum(drift, "rep") / replicas
    whole = [lax.all_gather(a, "rep", axis=0, tiled=True) for a in (momentum, global_weights)]
    moment = outer_beta * whole[0] + mean_drift
    updated = whole[1] - outer_rate * (mean_drift + outer_beta * moment)
    base = (mixing * (1.0 - learning_rate * weight_decay)) * weights + (1.0 - mixing) * updated
    at = lax.axis_index("rep") * size
    return (
        base,
        lax.dynamic_slice_in_dim(moment, at, size, 0),
        lax.dynamic_slice_in_dim(updated, at, size, 0),
    )


def after(first, then):
    return lax.optimization_barrier((first, then))[0]


def body(inputs, key_grads, weights, first_moment, second_moment, drift, momentum, global_weights):
    x, kg, master = inputs[0], key_grads[0], weights[0]
    tokens, depth = x.shape
    rows, columns = master.shape
    shards = lax.axis_size("fsdp")
    line = shards // 2
    swap = [(i, i ^ 1) for i in range(shards)]
    onward = [(i, i + 2) for i in range(0, shards - 2, 2)] + [(shards - 2, shards - 1)]
    onward += [(i, i - 2) for i in range(3, shards, 2)] + [(1, 0)]
    piece = array((rows, columns), BF16)
    cells = rows * columns
    summed_cost = cost(4 * tokens * cells, 6 * cells + 4 * tokens * rows)

    low = master.astype(BF16)
    first_a = lax.ppermute(low, "fsdp", onward)
    low_partner = lax.ppermute(low, "fsdp", swap)
    arrived = {1: (first_a, lax.ppermute(low_partner, "fsdp", onward))}
    xp = lax.ppermute(x, "fsdp", swap)
    kgp = lax.ppermute(kg, "fsdp", swap)

    unrotated, cosine, sines, total, other, input_grads = pl.pallas_call(
        functools.partial(local_kernel, line),
        out_shape=(
            array((2 * tokens, columns), BF16),
            array((tokens, HEAD), F32),
            array((tokens, HEAD), F32),
            array((2 * tokens, columns), F32),
            array((tokens, rows), BF16),
            array((tokens, depth), BF16),
        ),
        in_specs=[VMEM] * 5,
        out_specs=(VMEM,) * 5 + (ANY,),
        scratch_shapes=[pltpu.VMEM((tokens, rows), BF16), pltpu.SemaphoreType.DMA],
        compiler_params=PARAMS,
        cost_estimate=cost(8 * tokens * cells, 6 * cells),
        name="local",
    )(x, xp, kg, kgp, low)

    def step(slot, half, value):
        return pl.pallas_call(
            functools.partial(step_kernel, line, slot, half),
            out_shape=piece,
            in_specs=[VMEM] * 4,
            out_specs=VMEM,
            compiler_params=PARAMS,
            cost_estimate=summed_cost,
            name=f"step{slot}{'ab'[half]}",
        )(value, x, xp, unrotated)

    others = [lax.ppermute(other, "fsdp", swap)]

    def project_hop(hop, pieces, total, input_grads):
        wide = 2 * rows + (columns if hop == line - 1 else 0)
        return pl.pallas_call(
            functools.partial(project_kernel, line, hop),
            out_shape=(
                array((2 * tokens, columns), F32),
                array((tokens, wide), BF16),
                array((tokens, depth), BF16),
            ),
            in_specs=[VMEM] * 4 + [ANY] + [VMEM] * 2,
            out_specs=(VMEM, VMEM, ANY),
            scratch_shapes=[
                pltpu.VMEM((2, tokens, rows), BF16),
                pltpu.SemaphoreType.DMA((2,)),
            ],
            input_output_aliases={4: 2},
            compiler_params=PARAMS,
            cost_estimate=cost(16 * tokens * cells, 8 * cells),
            name=f"project{hop}",
        )(x, xp, unrotated, total, input_grads, *pieces)

    pairwise = lax.axis_size("rep") == 4
    delta = drift[0]
    if not pairwise:
        base, new_momentum, new_global = outer_plain(delta, momentum, global_weights, master)
    for slot in range(1, line):
        value = arrived[slot][0]
        if slot > 1:
            value = after(value, sent)
        sent = step(slot, 0, value)
        first = lax.ppermute(sent, "fsdp", onward)
        value = arrived[slot][1]
        if pairwise and slot == 1:
            packed, near = outer_pack(after(delta, sent), momentum, global_weights)
        if pairwise and slot == 2:
            repacked, far = outer_repack(after(delta, sent), packed, near)
        if pairwise and slot == 3:
            base, new_momentum, new_global = outer_end(
                after(delta, sent), near, far, momentum, global_weights, master
            )
        sent = step(slot, 1, after(value, sent))
        arrived[slot + 1] = (first, lax.ppermute(sent, "fsdp", onward))
        total, other, input_grads = project_hop(
            slot, arrived[slot], after(total, sent), input_grads
        )
        others.append(lax.ppermute(other, "fsdp", swap))
    sum_partner, sum_own = arrived[line]
    sum_swapped = lax.ppermute(after(sum_partner, sent), "fsdp", swap)

    summed = pl.pallas_call(
        functools.partial(early_kernel, line),
        out_shape=array((rows, columns), F32),
        in_specs=[VMEM] * 4,
        out_specs=VMEM,
        compiler_params=PARAMS,
        cost_estimate=cost(0, 0),
        name="early",
    )(x, xp, unrotated, sum_swapped)
    work = 2 * line - 1
    keys, input_grads = pl.pallas_call(
        functools.partial(merge_kernel, line),
        out_shape=(array((tokens, columns), BF16), array((tokens, depth), BF16)),
        in_specs=[VMEM] * 3 + [ANY] * (1 + line),
        out_specs=(VMEM, ANY),
        scratch_shapes=[
            pltpu.VMEM((tokens, columns), BF16),
            pltpu.SemaphoreType.DMA((work,)),
            pltpu.SemaphoreType.DMA,
        ],
        input_output_aliases={3: 1},
        compiler_params=PARAMS,
        cost_estimate=cost(0, 0),
        name="merge",
    )(cosine, sines, after(total, summed), input_grads, *others)
    sum_own = after(sum_own, keys)
    merged, first_out, second_out = pl.pallas_call(
        functools.partial(update_kernel, line),
        out_shape=(
            array((rows, columns), F32),
            array((rows, columns), BF16),
            array((rows, columns), BF16),
        ),
        in_specs=[VMEM] * 5,
        out_specs=(ANY,) * 3,
        scratch_shapes=[
            pltpu.VMEM((rows, columns), F32),
            pltpu.VMEM((rows, columns), BF16),
            pltpu.VMEM((rows, columns), BF16),
            pltpu.SemaphoreType.DMA((4, 3)),
        ],
        compiler_params=PARAMS,
        cost_estimate=cost(20 * cells, 18 * cells),
        name="update",
    )(summed, sum_own, first_moment[0], second_moment[0], base)
    return (
        keys[None],
        input_grads[None],
        merged[None],
        first_out[None],
        second_out[None],
        new_momentum,
        new_global,
    )


def solution(mesh):
    sharded = P("rep", "fsdp", None)
    rows = P(("fsdp", "rep"), None)
    return jax.shard_map(
        body,
        mesh=mesh,
        in_specs=(sharded,) * 6 + (rows,) * 2,
        out_specs=(sharded,) * 5 + (rows,) * 2,
        check_vma=False,
    )
```

```python
import functools

import jax
import jax.numpy as jnp
from jax import lax
from jax.experimental import pallas as pl
from jax.experimental.pallas import tpu as pltpu
from jax.sharding import PartitionSpec as P

HEAD = 128
SEQ = 1024

learning_rate = 0.002
beta_one = 0.9
beta_two = 0.95
adam_epsilon = 1e-08
weight_decay = 0.1
outer_rate = 0.7
outer_beta = 0.9
mixing = 0.5
rope_base = 500000.0

VMEM = pl.BlockSpec(memory_space=pltpu.VMEM)
ANY = pl.BlockSpec(memory_space=pl.ANY)
PARAMS = pltpu.CompilerParams(vmem_limit_bytes=10 * 1024 * 1024)
F32 = jnp.float32
BF16 = jnp.bfloat16


def array(shape, kind):
    return jax.ShapeDtypeStruct(shape, kind)


def cost(flops, bytes_accessed):
    return pl.CostEstimate(
        flops=30 * flops, bytes_accessed=30 * bytes_accessed, transcendentals=0
    )


def position(line):
    shard = lax.axis_index("fsdp")
    place, core = lax.div(shard, 2), lax.rem(shard, 2)
    ahead = 1 - 2 * core
    behind = jnp.where(core == 0, place, line - 1 - place)
    return place, core, ahead, behind


def block_at(place, parity, rows):
    return pl.multiple_of((2 * place + parity) * rows, 128)


def rotate_block(values, cosine, sines):
    heads = []
    for at in range(0, values.shape[1], HEAD):
        head = values[:, at : at + HEAD]
        heads.append(head * cosine + pltpu.roll(head, HEAD // 2, 1) * sines)
    return jnp.concatenate(heads, axis=1)


def rope_tables(shard, tokens):
    half_size = HEAD // 2
    token = lax.broadcasted_iota(jnp.int32, (tokens, HEAD), 0)
    column = lax.broadcasted_iota(jnp.int32, (tokens, HEAD), 1)
    exponents = lax.rem(column, half_size).astype(F32) * (2.0 / HEAD)
    inverse_freq = jnp.power(F32(rope_base), -exponents)
    angles = lax.rem(shard * tokens + token, SEQ).astype(F32) * inverse_freq
    sines = jnp.sin(angles)
    return jnp.cos(angles), jnp.where(column < half_size, -sines, sines)


def gradient_term(x, xp, unrotated, at, size):
    columns = pl.ds(at, size)
    left = jnp.concatenate([x[:, columns], xp[:, columns]], axis=0)
    return lax.dot_general(
        left, unrotated[...], (((0,), (0,)), ((), ())), preferred_element_type=F32
    )


def project(x, xp, unrotated, piece, total, stage, other, at, grads, sem):
    columns = pl.ds(at, piece.shape[0])
    tokens = x.shape[0]
    both = jnp.concatenate([x[:, columns], xp[:, columns]], axis=0)
    total[...] += jnp.dot(both, piece[...], preferred_element_type=F32)
    made = lax.dot_general(
        unrotated[...], piece[...], (((1,), (1,)), ((), ())), preferred_element_type=F32
    ).astype(BF16)
    stage[...] = made[:tokens, :]
    other[...] = made[tokens:, :]
    pltpu.make_async_copy(stage, grads.at[:, columns], sem).start()


def project_wait(stage, grads, at, sem):
    pltpu.make_async_copy(stage, grads.at[:, pl.ds(at, stage.shape[1])], sem).wait()


def local_kernel(line, x, xp, kg, kgp, low, *refs):
    unrotated, cosine, sines, total, other, grads, stage, sem = refs
    tokens = x.shape[0]
    place, core, _, _ = position(line)
    shard = 2 * place + core
    for half, source in enumerate((kg, kgp)):
        cosines, signed = rope_tables(jnp.bitwise_xor(shard, half), tokens)
        unrotated[half * tokens : (half + 1) * tokens, :] = rotate_block(
            source[...].astype(F32), cosines, -signed
        ).astype(BF16)
        if half == 0:
            cosine[...] = cosines
            sines[...] = signed
    total[...] = jnp.zeros_like(total)
    at = block_at(place, core, low.shape[0])
    project(x, xp, unrotated, low, total, stage, other, at, grads, sem)
    project_wait(stage, grads, at, sem)


def project_kernel(line, hop, x, xp, unrotated, total_in, grads_in, *refs):
    del grads_in
    first, second, total, other, grads, stage, sems = refs
    tokens = x.shape[0]
    rows = first.shape[0]
    place, core, ahead, behind = position(line)
    total[...] = total_in[...]

    @pl.when(behind >= hop)
    def _():
        work = [(first, core), (second, 1 - core)]
        ats = [block_at(place - hop * ahead, parity, rows) for _, parity in work]
        for i, (piece, _) in enumerate(work):
            into = other.at[:, i * rows : (i + 1) * rows]
            project(
                x, xp, unrotated, piece, total, stage.at[i], into, ats[i], grads, sems.at[i]
            )
        for i in range(2):
            project_wait(stage.at[i], grads, ats[i], sems.at[i])

    if hop == line - 1:
        other[:, 2 * rows :] = total[tokens:, :].astype(BF16)


def merge_kernel(line, cosine, sines, total, grads_in, *refs):
    del grads_in
    others = refs[:line]
    keys, grads, partial, sems, sem = refs[line:]
    tokens, _ = keys.shape
    rows = others[0].shape[1]
    place, core, ahead, behind = position(line)
    work = [(behind >= 0, place, 1 - core, others[0].at[:, :])]
    for hop in range(1, line):
        for i, parity in enumerate((1 - core, core)):
            part = others[hop].at[:, i * rows : (i + 1) * rows]
            work.append((behind + hop < line, place + hop * ahead, parity, part))

    def copy(i):
        _, owner, parity, part = work[i]
        at = pl.ds(block_at(owner, parity, rows), rows)
        return pltpu.make_async_copy(part, grads.at[:, at], sems.at[i])

    rest = pltpu.make_async_copy(others[line - 1].at[:, 2 * rows :], partial, sem)
    rest.start()
    for i in range(len(work)):
        pl.when(work[i][0])(lambda i=i: copy(i).start())
    rest.wait()
    keys[...] = rotate_block(
        total[:tokens, :] + partial[...].astype(F32), cosine[...], sines[...]
    ).astype(BF16)
    for i in range(len(work)):
        pl.when(work[i][0])(lambda i=i: copy(i).wait())


def step_kernel(line, slot, half, arrived, x, xp, unrotated, *parts):
    place, core, ahead, behind = position(line)
    rows = arrived.shape[0]
    part = parts[0].shape[0]
    size = min(part, 256)
    parity = core if half else 1 - core

    @pl.when(behind >= slot)
    def _():
        for i, sent in enumerate(parts):
            sent[...] = arrived[i * part : (i + 1) * part, :]

    @pl.when(behind < slot)
    def _():
        owner = place + (line - slot) * ahead
        for at in range(0, rows, size):
            term = gradient_term(
                x, xp, unrotated, pl.multiple_of(block_at(owner, parity, rows) + at, 128), size
            )
            before = arrived[at : at + size, :].astype(F32)
            total = (term + jnp.where(behind > 0, before, 0.0)).astype(BF16)
            parts[at // part][at % part : at % part + size, :] = total


def update_kernel(line, start, x, xp, unrotated, swapped, arrived, first, second, base, *refs):
    merged, first_out, second_out, summed, merged_v, first_v, second_v, sem = refs[-8:]
    place, core, _, behind = position(line)
    own_at = block_at(place, core, first.shape[0])
    summed[...] = gradient_term(
        x, xp, unrotated, pl.multiple_of(own_at + start, 128), arrived.shape[0]
    )
    parts = sem.shape[0]
    size = arrived.shape[0] // parts
    chunk = min(size, 32)
    outs = ((merged_v, merged), (first_v, first_out), (second_v, second_out))

    def copies(part):
        return [
            pltpu.make_async_copy(
                source.at[pl.ds(part * size, size), :],
                target.at[pl.ds(start + part * size, size), :],
                sem.at[part, i],
            )
            for i, (source, target) in enumerate(outs)
        ]

    for part in range(parts):

        def some(i, carry, part=part):
            own = pl.multiple_of(part * size + i * chunk, 16)
            here, at = pl.ds(own, chunk), pl.ds(start + own, chunk)
            near = jnp.where(behind < line - 1, swapped[at, :].astype(F32), 0.0)
            last = jnp.where(behind > 0, arrived[here, :].astype(F32), 0.0)
            gradient = summed[here, :] + near + last
            one = beta_one * first[at, :].astype(F32) + (1.0 - beta_one) * gradient
            two = beta_two * second[at, :].astype(F32) + (1.0 - beta_two) * gradient * gradient
            inverse = lax.rsqrt(two)
            step = one * (inverse * (2.0 - (two * inverse + adam_epsilon) * inverse))
            merged_v[here, :] = base[at, :] - (mixing * learning_rate) * step
            first_v[here, :] = one.astype(BF16)
            second_v[here, :] = two.astype(BF16)
            return carry

        lax.fori_loop(0, size // chunk, some, 0, unroll=True)
        for copy in copies(part):
            copy.start()
    for part in range(parts):
        for copy in copies(part):
            copy.wait()


outer_held = outer_rate * outer_beta * outer_beta
outer_slope = outer_rate * (1.0 + outer_beta)


def pack_kernel(drift, momentum, global_weights, packed):
    rows = drift.shape[0]
    packed[:rows, :] = drift[...].astype(BF16)
    packed[rows:, :] = (global_weights[...] - outer_held * momentum[...]).astype(BF16)


def repack_kernel(drift, mine, other, packed):
    rows = drift.shape[0]
    size = mine.shape[0] - rows
    packed[:rows, :] = (drift[...] + other[:rows, :].astype(F32)).astype(BF16)
    packed[rows : rows + size, :] = mine[rows:, :]
    packed[rows + size :, :] = other[rows:, :]


def outer_kernel(drift, near, far, momentum, global_weights, weights, *refs):
    base, new_momentum, new_global = refs
    rows = drift.shape[0]
    size = momentum.shape[0]
    replica = lax.axis_index("rep")
    core = lax.rem(lax.axis_index("fsdp"), 2)
    held = (None, near.at[rows:, :], far.at[rows : rows + size, :], far.at[rows + size :, :])
    for shift, other in enumerate((0, 1 + core, 2 - core, 3)):
        at = pl.ds(pl.multiple_of(jnp.bitwise_xor(replica, other) * size, size), size)
        total = drift[at, :] + near[at, :].astype(F32) + far[at, :].astype(F32)
        mean_drift = total / 4
        if shift == 0:
            moment = outer_beta * momentum[...] + mean_drift
            updated = global_weights[...] - outer_rate * (mean_drift + outer_beta * moment)
            new_momentum[...] = moment
            new_global[...] = updated
        else:
            updated = held[shift][...].astype(F32) - outer_slope * mean_drift
        base[at, :] = (mixing * (1.0 - learning_rate * weight_decay)) * weights[at, :] + (
            1.0 - mixing
        ) * updated


def pairs_of(turn, shards):
    return [
        (i * shards + j, (i ^ (1 + (j + turn) % 2)) * shards + j)
        for i in range(4)
        for j in range(shards)
    ]


def outer_pack(drift, momentum, global_weights):
    rows, columns = drift.shape
    packed = pl.pallas_call(
        pack_kernel,
        out_shape=array((rows + momentum.shape[0], columns), BF16),
        in_specs=[VMEM] * 3,
        out_specs=VMEM,
        compiler_params=PARAMS,
        cost_estimate=cost(0, 0),
        name="pack",
    )(drift, momentum, global_weights)
    near = lax.ppermute(packed, ("rep", "fsdp"), pairs_of(0, lax.axis_size("fsdp")))
    return packed, near


def outer_repack(drift, packed, near):
    rows, columns = drift.shape
    repacked = pl.pallas_call(
        repack_kernel,
        out_shape=array((2 * packed.shape[0] - rows, columns), BF16),
        in_specs=[VMEM] * 3,
        out_specs=VMEM,
        compiler_params=PARAMS,
        cost_estimate=cost(0, 0),
        name="repack",
    )(drift, packed, near)
    return repacked, lax.ppermute(repacked, ("rep", "fsdp"), pairs_of(1, lax.axis_size("fsdp")))


def outer_end(drift, near, far, momentum, global_weights, weights):
    rows, columns = drift.shape
    size = momentum.shape[0]
    return pl.pallas_call(
        outer_kernel,
        out_shape=(
            array((rows, columns), F32),
            array((size, columns), F32),
            array((size, columns), F32),
        ),
        in_specs=[VMEM] * 6,
        out_specs=(VMEM,) * 3,
        compiler_params=PARAMS,
        cost_estimate=cost(0, 0),
        name="outer",
    )(drift, near, far, momentum, global_weights, weights)


def outer_plain(drift, momentum, global_weights, weights):
    replicas = lax.axis_size("rep")
    size = momentum.shape[0]
    mean_drift = lax.psum(drift, "rep") / replicas
    whole = [lax.all_gather(a, "rep", axis=0, tiled=True) for a in (momentum, global_weights)]
    moment = outer_beta * whole[0] + mean_drift
    updated = whole[1] - outer_rate * (mean_drift + outer_beta * moment)
    base = (mixing * (1.0 - learning_rate * weight_decay)) * weights + (1.0 - mixing) * updated
    at = lax.axis_index("rep") * size
    return (
        base,
        lax.dynamic_slice_in_dim(moment, at, size, 0),
        lax.dynamic_slice_in_dim(updated, at, size, 0),
    )


def after(first, then):
    return lax.optimization_barrier((first, then))[0]


def body(inputs, key_grads, weights, first_moment, second_moment, drift, momentum, global_weights):
    x, kg, master = inputs[0], key_grads[0], weights[0]
    tokens, depth = x.shape
    rows, columns = master.shape
    shards = lax.axis_size("fsdp")
    line = shards // 2
    swap = [(i, i ^ 1) for i in range(shards)]
    onward = [(i, i + 2) for i in range(0, shards - 2, 2)] + [(shards - 2, shards - 1)]
    onward += [(i, i - 2) for i in range(3, shards, 2)] + [(1, 0)]
    across = [(i, j ^ 1) for i, j in onward]
    piece = array((rows, columns), BF16)
    cells = rows * columns
    summed_cost = cost(4 * tokens * cells, 6 * cells + 4 * tokens * rows)

    low = master.astype(BF16)
    first_a = lax.ppermute(low, "fsdp", onward)
    low_partner = lax.ppermute(low, "fsdp", swap)
    arrived = {1: (first_a, lax.ppermute(low_partner, "fsdp", onward))}
    xp = lax.ppermute(x, "fsdp", swap)
    kgp = lax.ppermute(kg, "fsdp", swap)

    unrotated, cosine, sines, total, other, input_grads = pl.pallas_call(
        functools.partial(local_kernel, line),
        out_shape=(
            array((2 * tokens, columns), BF16),
            array((tokens, HEAD), F32),
            array((tokens, HEAD), F32),
            array((2 * tokens, columns), F32),
            array((tokens, rows), BF16),
            array((tokens, depth), BF16),
        ),
        in_specs=[VMEM] * 5,
        out_specs=(VMEM,) * 5 + (ANY,),
        scratch_shapes=[pltpu.VMEM((tokens, rows), BF16), pltpu.SemaphoreType.DMA],
        compiler_params=PARAMS,
        cost_estimate=cost(8 * tokens * cells, 6 * cells),
        name="local",
    )(x, xp, kg, kgp, low)

    last_parts = 2 if rows % 64 == 0 else 1

    def step(slot, half, value):
        parts = last_parts if slot == line - 1 and half else 1
        return pl.pallas_call(
            functools.partial(step_kernel, line, slot, half),
            out_shape=(array((rows // parts, columns), BF16),) * parts,
            in_specs=[VMEM] * 4,
            out_specs=(VMEM,) * parts,
            compiler_params=PARAMS,
            cost_estimate=cost(0, 0) if slot == line - 1 else summed_cost,
            name=f"step{slot}{'ab'[half]}",
        )(value, x, xp, unrotated)

    others = [lax.ppermute(other, "fsdp", swap)]

    def project_hop(hop, pieces, total, input_grads):
        wide = 2 * rows + (columns if hop == line - 1 else 0)
        return pl.pallas_call(
            functools.partial(project_kernel, line, hop),
            out_shape=(
                array((2 * tokens, columns), F32),
                array((tokens, wide), BF16),
                array((tokens, depth), BF16),
            ),
            in_specs=[VMEM] * 4 + [ANY] + [VMEM] * 2,
            out_specs=(VMEM, VMEM, ANY),
            scratch_shapes=[
                pltpu.VMEM((2, tokens, rows), BF16),
                pltpu.SemaphoreType.DMA((2,)),
            ],
            input_output_aliases={4: 2},
            compiler_params=PARAMS,
            cost_estimate=cost(0, 0) if hop == line - 1 else cost(16 * tokens * cells, 8 * cells),
            name=f"project{hop}",
        )(x, xp, unrotated, total, input_grads, *pieces)

    pairwise = lax.axis_size("rep") == 4
    delta = drift[0]
    if not pairwise:
        base, new_momentum, new_global = outer_plain(delta, momentum, global_weights, master)
    for slot in range(1, line):
        value = arrived[slot][0]
        if slot > 1:
            value = after(value, sent)
        (sent,) = step(slot, 0, value)
        first = lax.ppermute(sent, "fsdp", across if slot == line - 1 else onward)
        value = arrived[slot][1]
        if pairwise and slot == 1:
            packed, near = outer_pack(after(delta, sent), momentum, global_weights)
        if pairwise and slot == 2:
            repacked, far = outer_repack(after(delta, sent), packed, near)
        if pairwise and slot == 3:
            base, new_momentum, new_global = outer_end(
                after(delta, sent), near, far, momentum, global_weights, master
            )
        waits = [sent, others] if slot == line - 1 else sent
        sent, *rest = step(slot, 1, after(value, waits))
        second = [lax.ppermute(part, "fsdp", onward) for part in (sent, *rest)]
        arrived[slot + 1] = (first, second if rest else second[0])
        total, other, input_grads = project_hop(
            slot, arrived[slot], after(total, sent), input_grads
        )
        others.append(lax.ppermute(other, "fsdp", swap))
    sum_swapped, sum_own = arrived[line]

    work = 2 * line - 1
    keys, input_grads = pl.pallas_call(
        functools.partial(merge_kernel, line),
        out_shape=(array((tokens, columns), BF16), array((tokens, depth), BF16)),
        in_specs=[VMEM] * 3 + [ANY] * (1 + line),
        out_specs=(VMEM, ANY),
        scratch_shapes=[
            pltpu.VMEM((tokens, columns), BF16),
            pltpu.SemaphoreType.DMA((work,)),
            pltpu.SemaphoreType.DMA,
        ],
        input_output_aliases={3: 1},
        compiler_params=PARAMS,
        cost_estimate=cost(0, 0),
        name="merge",
    )(cosine, sines, total, input_grads, *others)
    if last_parts == 1:
        sum_own = [sum_own]
    results = ()
    for i, part in enumerate(sum_own):
        size = part.shape[0]
        pieces = 4 if size % 128 == 0 else 1
        if i == 0:
            part = after(part, keys)
        results = pl.pallas_call(
            functools.partial(update_kernel, line, i * size),
            out_shape=(
                array((rows, columns), F32),
                array((rows, columns), BF16),
                array((rows, columns), BF16),
            ),
            in_specs=[VMEM] * 8 + [ANY] * len(results),
            out_specs=(ANY,) * 3,
            scratch_shapes=[
                pltpu.VMEM((size, columns), F32),
                pltpu.VMEM((size, columns), F32),
                pltpu.VMEM((size, columns), BF16),
                pltpu.VMEM((size, columns), BF16),
                pltpu.SemaphoreType.DMA((pieces, 3)),
            ],
            input_output_aliases={8 + j: j for j in range(len(results))},
            compiler_params=PARAMS,
            cost_estimate=cost(0, 0),
            name=f"update{i}",
        )(x, xp, unrotated, sum_swapped, part, first_moment[0], second_moment[0], base, *results)
    merged, first_out, second_out = results
    return (
        keys[None],
        input_grads[None],
        merged[None],
        first_out[None],
        second_out[None],
        new_momentum,
        new_global,
    )


def solution(mesh):
    sharded = P("rep", "fsdp", None)
    rows = P(("fsdp", "rep"), None)
    return jax.shard_map(
        body,
        mesh=mesh,
        in_specs=(sharded,) * 6 + (rows,) * 2,
        out_specs=(sharded,) * 5 + (rows,) * 2,
        check_vma=False,
    )
```

```python
import functools

import jax
import jax.numpy as jnp
from jax import lax
from jax.experimental import pallas as pl
from jax.experimental.pallas import tpu as pltpu
from jax.sharding import PartitionSpec as P

HEAD = 128
SEQ = 1024

learning_rate = 0.002
beta_one = 0.9
beta_two = 0.95
adam_epsilon = 1e-08
weight_decay = 0.1
outer_rate = 0.7
outer_beta = 0.9
mixing = 0.5
rope_base = 500000.0

VMEM = pl.BlockSpec(memory_space=pltpu.VMEM)
ANY = pl.BlockSpec(memory_space=pl.ANY)
PARAMS = pltpu.CompilerParams(vmem_limit_bytes=10 * 1024 * 1024)
F32 = jnp.float32
BF16 = jnp.bfloat16


def array(shape, kind):
    return jax.ShapeDtypeStruct(shape, kind)


def cost(flops, bytes_accessed):
    return pl.CostEstimate(
        flops=30 * flops, bytes_accessed=30 * bytes_accessed, transcendentals=0
    )


def position(line):
    shard = lax.axis_index("fsdp")
    place, core = lax.div(shard, 2), lax.rem(shard, 2)
    ahead = 1 - 2 * core
    behind = jnp.where(core == 0, place, line - 1 - place)
    return place, core, ahead, behind


def block_at(place, parity, rows):
    return pl.multiple_of((2 * place + parity) * rows, 128)


def rotate_block(values, cosine, sines):
    heads = []
    for at in range(0, values.shape[1], HEAD):
        head = values[:, at : at + HEAD]
        heads.append(head * cosine + pltpu.roll(head, HEAD // 2, 1) * sines)
    return jnp.concatenate(heads, axis=1)


def rope_tables(shard, tokens):
    half_size = HEAD // 2
    token = lax.broadcasted_iota(jnp.int32, (tokens, HEAD), 0)
    column = lax.broadcasted_iota(jnp.int32, (tokens, HEAD), 1)
    exponents = lax.rem(column, half_size).astype(F32) * (2.0 / HEAD)
    inverse_freq = jnp.power(F32(rope_base), -exponents)
    angles = lax.rem(shard * tokens + token, SEQ).astype(F32) * inverse_freq
    sines = jnp.sin(angles)
    return jnp.cos(angles), jnp.where(column < half_size, -sines, sines)


def gradient_term(x, xp, unrotated, at, size):
    columns = pl.ds(at, size)
    left = jnp.concatenate([x[:, columns], xp[:, columns]], axis=0)
    return lax.dot_general(
        left, unrotated[...], (((0,), (0,)), ((), ())), preferred_element_type=F32
    )


def project(x, xp, unrotated, piece, total, stage, other, at, grads, sem):
    columns = pl.ds(at, piece.shape[0])
    tokens = x.shape[0]
    both = jnp.concatenate([x[:, columns], xp[:, columns]], axis=0)
    total[...] += jnp.dot(both, piece[...], preferred_element_type=F32)
    made = lax.dot_general(
        unrotated[...], piece[...], (((1,), (1,)), ((), ())), preferred_element_type=F32
    ).astype(BF16)
    stage[...] = made[:tokens, :]
    other[...] = made[tokens:, :]
    pltpu.make_async_copy(stage, grads.at[:, columns], sem).start()


def project_wait(stage, grads, at, sem):
    pltpu.make_async_copy(stage, grads.at[:, pl.ds(at, stage.shape[1])], sem).wait()


def local_kernel(line, x, xp, kg, kgp, low, *refs):
    unrotated, cosine, sines, total, other, grads, stage, sem = refs
    tokens = x.shape[0]
    place, core, _, _ = position(line)
    shard = 2 * place + core
    for half, source in enumerate((kg, kgp)):
        cosines, signed = rope_tables(jnp.bitwise_xor(shard, half), tokens)
        unrotated[half * tokens : (half + 1) * tokens, :] = rotate_block(
            source[...].astype(F32), cosines, -signed
        ).astype(BF16)
        if half == 0:
            cosine[...] = cosines
            sines[...] = signed
    total[...] = jnp.zeros_like(total)
    at = block_at(place, core, low.shape[0])
    project(x, xp, unrotated, low, total, stage, other, at, grads, sem)
    project_wait(stage, grads, at, sem)


def project_kernel(line, hop, x, xp, unrotated, total_in, grads_in, *refs):
    del grads_in
    first, second, total, other, grads, stage, sems = refs
    tokens = x.shape[0]
    rows = first.shape[0]
    place, core, ahead, behind = position(line)
    total[...] = total_in[...]

    @pl.when(behind >= hop)
    def _():
        work = [(first, core), (second, 1 - core)]
        ats = [block_at(place - hop * ahead, parity, rows) for _, parity in work]
        for i, (piece, _) in enumerate(work):
            into = other.at[:, i * rows : (i + 1) * rows]
            project(
                x, xp, unrotated, piece, total, stage.at[i], into, ats[i], grads, sems.at[i]
            )
        for i in range(2):
            project_wait(stage.at[i], grads, ats[i], sems.at[i])

    if hop == line - 1:
        other[:, 2 * rows :] = total[tokens:, :].astype(BF16)


def merge_kernel(line, cosine, sines, total, grads_in, *refs):
    del grads_in
    others = refs[:line]
    keys, grads, partial, sems, sem = refs[line:]
    tokens, _ = keys.shape
    rows = others[0].shape[1]
    place, core, ahead, behind = position(line)
    work = [(behind >= 0, place, 1 - core, others[0].at[:, :])]
    for hop in range(1, line):
        for i, parity in enumerate((1 - core, core)):
            part = others[hop].at[:, i * rows : (i + 1) * rows]
            work.append((behind + hop < line, place + hop * ahead, parity, part))

    def copy(i):
        _, owner, parity, part = work[i]
        at = pl.ds(block_at(owner, parity, rows), rows)
        return pltpu.make_async_copy(part, grads.at[:, at], sems.at[i])

    rest = pltpu.make_async_copy(others[line - 1].at[:, 2 * rows :], partial, sem)
    rest.start()
    for i in range(len(work)):
        pl.when(work[i][0])(lambda i=i: copy(i).start())
    rest.wait()
    keys[...] = rotate_block(
        total[:tokens, :] + partial[...].astype(F32), cosine[...], sines[...]
    ).astype(BF16)
    for i in range(len(work)):
        pl.when(work[i][0])(lambda i=i: copy(i).wait())


def step_kernel(line, slot, half, arrived, x, xp, unrotated, sent):
    place, core, ahead, behind = position(line)
    rows = arrived.shape[0]
    size = min(rows, 256)
    parity = core if half else 1 - core

    @pl.when(behind >= slot)
    def _():
        sent[...] = arrived[...]

    @pl.when(behind < slot)
    def _():
        owner = place + (line - slot) * ahead
        for at in range(0, rows, size):
            term = gradient_term(
                x, xp, unrotated, pl.multiple_of(block_at(owner, parity, rows) + at, 128), size
            )
            before = arrived[at : at + size, :].astype(F32)
            sent[at : at + size, :] = (term + jnp.where(behind > 0, before, 0.0)).astype(BF16)


def early_kernel(line, x, xp, unrotated, swapped, summed):
    place, core, _, behind = position(line)
    rows = swapped.shape[0]
    size = min(rows, 256)
    for at in range(0, rows, size):
        term = gradient_term(
            x, xp, unrotated, pl.multiple_of(block_at(place, core, rows) + at, 128), size
        )
        other = swapped[at : at + size, :].astype(F32)
        summed[at : at + size, :] = term + jnp.where(behind < line - 1, other, 0.0)


def update_kernel(line, summed, arrived, first, second, base, merged, first_out, second_out, *scratch):
    merged_v, first_v, second_v, sem = scratch
    behind = position(line)[3]
    rows = summed.shape[0]
    parts = 4
    size = rows // parts
    chunk = min(size, 32)
    outs = ((merged_v, merged), (first_v, first_out), (second_v, second_out))

    def copies(part):
        at = pl.ds(part * size, size)
        return [
            pltpu.make_async_copy(source.at[at, :], target.at[at, :], sem.at[part, i])
            for i, (source, target) in enumerate(outs)
        ]

    for part in range(parts):

        def some(i, carry, part=part):
            at = pl.ds(pl.multiple_of(part * size + i * chunk, 16), chunk)
            gradient = summed[at, :] + jnp.where(behind > 0, arrived[at, :].astype(F32), 0.0)
            one = beta_one * first[at, :].astype(F32) + (1.0 - beta_one) * gradient
            two = beta_two * second[at, :].astype(F32) + (1.0 - beta_two) * gradient * gradient
            inverse = lax.rsqrt(two)
            step = one * (inverse * (2.0 - (two * inverse + adam_epsilon) * inverse))
            merged_v[at, :] = base[at, :] - (mixing * learning_rate) * step
            first_v[at, :] = one.astype(BF16)
            second_v[at, :] = two.astype(BF16)
            return carry

        lax.fori_loop(0, size // chunk, some, 0, unroll=True)
        for copy in copies(part):
            copy.start()
    for part in range(parts):
        for copy in copies(part):
            copy.wait()


outer_held = outer_rate * outer_beta * outer_beta
outer_slope = outer_rate * (1.0 + outer_beta)


def pack_kernel(drift, momentum, global_weights, packed):
    rows = drift.shape[0]
    packed[:rows, :] = drift[...].astype(BF16)
    packed[rows:, :] = (global_weights[...] - outer_held * momentum[...]).astype(BF16)


def repack_kernel(drift, mine, other, packed):
    rows = drift.shape[0]
    size = mine.shape[0] - rows
    packed[:rows, :] = (drift[...] + other[:rows, :].astype(F32)).astype(BF16)
    packed[rows : rows + size, :] = mine[rows:, :]
    packed[rows + size :, :] = other[rows:, :]


def outer_kernel(drift, near, far, momentum, global_weights, weights, *refs):
    base, new_momentum, new_global = refs
    rows = drift.shape[0]
    size = momentum.shape[0]
    replica = lax.axis_index("rep")
    core = lax.rem(lax.axis_index("fsdp"), 2)
    held = (None, near.at[rows:, :], far.at[rows : rows + size, :], far.at[rows + size :, :])
    for shift, other in enumerate((0, 1 + core, 2 - core, 3)):
        at = pl.ds(pl.multiple_of(jnp.bitwise_xor(replica, other) * size, size), size)
        total = drift[at, :] + near[at, :].astype(F32) + far[at, :].astype(F32)
        mean_drift = total / 4
        if shift == 0:
            moment = outer_beta * momentum[...] + mean_drift
            updated = global_weights[...] - outer_rate * (mean_drift + outer_beta * moment)
            new_momentum[...] = moment
            new_global[...] = updated
        else:
            updated = held[shift][...].astype(F32) - outer_slope * mean_drift
        base[at, :] = (mixing * (1.0 - learning_rate * weight_decay)) * weights[at, :] + (
            1.0 - mixing
        ) * updated


def pairs_of(turn, shards):
    return [
        (i * shards + j, (i ^ (1 + (j + turn) % 2)) * shards + j)
        for i in range(4)
        for j in range(shards)
    ]


def outer_pack(drift, momentum, global_weights):
    rows, columns = drift.shape
    packed = pl.pallas_call(
        pack_kernel,
        out_shape=array((rows + momentum.shape[0], columns), BF16),
        in_specs=[VMEM] * 3,
        out_specs=VMEM,
        compiler_params=PARAMS,
        cost_estimate=cost(0, 0),
        name="pack",
    )(drift, momentum, global_weights)
    near = lax.ppermute(packed, ("rep", "fsdp"), pairs_of(0, lax.axis_size("fsdp")))
    return packed, near


def outer_repack(drift, packed, near):
    rows, columns = drift.shape
    repacked = pl.pallas_call(
        repack_kernel,
        out_shape=array((2 * packed.shape[0] - rows, columns), BF16),
        in_specs=[VMEM] * 3,
        out_specs=VMEM,
        compiler_params=PARAMS,
        cost_estimate=cost(0, 0),
        name="repack",
    )(drift, packed, near)
    return repacked, lax.ppermute(repacked, ("rep", "fsdp"), pairs_of(1, lax.axis_size("fsdp")))


def outer_end(drift, near, far, momentum, global_weights, weights):
    rows, columns = drift.shape
    size = momentum.shape[0]
    return pl.pallas_call(
        outer_kernel,
        out_shape=(
            array((rows, columns), F32),
            array((size, columns), F32),
            array((size, columns), F32),
        ),
        in_specs=[VMEM] * 6,
        out_specs=(VMEM,) * 3,
        compiler_params=PARAMS,
        cost_estimate=cost(0, 0),
        name="outer",
    )(drift, near, far, momentum, global_weights, weights)


def outer_plain(drift, momentum, global_weights, weights):
    replicas = lax.axis_size("rep")
    size = momentum.shape[0]
    mean_drift = lax.psum(drift, "rep") / replicas
    whole = [lax.all_gather(a, "rep", axis=0, tiled=True) for a in (momentum, global_weights)]
    moment = outer_beta * whole[0] + mean_drift
    updated = whole[1] - outer_rate * (mean_drift + outer_beta * moment)
    base = (mixing * (1.0 - learning_rate * weight_decay)) * weights + (1.0 - mixing) * updated
    at = lax.axis_index("rep") * size
    return (
        base,
        lax.dynamic_slice_in_dim(moment, at, size, 0),
        lax.dynamic_slice_in_dim(updated, at, size, 0),
    )


def after(first, then):
    return lax.optimization_barrier((first, then))[0]


def body(inputs, key_grads, weights, first_moment, second_moment, drift, momentum, global_weights):
    x, kg, master = inputs[0], key_grads[0], weights[0]
    tokens, depth = x.shape
    rows, columns = master.shape
    shards = lax.axis_size("fsdp")
    line = shards // 2
    swap = [(i, i ^ 1) for i in range(shards)]
    onward = [(i, i + 2) for i in range(0, shards - 2, 2)] + [(shards - 2, shards - 1)]
    onward += [(i, i - 2) for i in range(3, shards, 2)] + [(1, 0)]
    piece = array((rows, columns), BF16)
    cells = rows * columns
    summed_cost = cost(4 * tokens * cells, 6 * cells + 4 * tokens * rows)

    low = master.astype(BF16)
    first_a = lax.ppermute(low, "fsdp", onward)
    low_partner = lax.ppermute(low, "fsdp", swap)
    arrived = {1: (first_a, lax.ppermute(low_partner, "fsdp", onward))}
    xp = lax.ppermute(x, "fsdp", swap)
    kgp = lax.ppermute(kg, "fsdp", swap)

    unrotated, cosine, sines, total, other, input_grads = pl.pallas_call(
        functools.partial(local_kernel, line),
        out_shape=(
            array((2 * tokens, columns), BF16),
            array((tokens, HEAD), F32),
            array((tokens, HEAD), F32),
            array((2 * tokens, columns), F32),
            array((tokens, rows), BF16),
            array((tokens, depth), BF16),
        ),
        in_specs=[VMEM] * 5,
        out_specs=(VMEM,) * 5 + (ANY,),
        scratch_shapes=[pltpu.VMEM((tokens, rows), BF16), pltpu.SemaphoreType.DMA],
        compiler_params=PARAMS,
        cost_estimate=cost(8 * tokens * cells, 6 * cells),
        name="local",
    )(x, xp, kg, kgp, low)

    def step(slot, half, value):
        return pl.pallas_call(
            functools.partial(step_kernel, line, slot, half),
            out_shape=piece,
            in_specs=[VMEM] * 4,
            out_specs=VMEM,
            compiler_params=PARAMS,
            cost_estimate=summed_cost,
            name=f"step{slot}{'ab'[half]}",
        )(value, x, xp, unrotated)

    others = [lax.ppermute(other, "fsdp", swap)]

    def project_hop(hop, pieces, total, input_grads):
        wide = 2 * rows + (columns if hop == line - 1 else 0)
        return pl.pallas_call(
            functools.partial(project_kernel, line, hop),
            out_shape=(
                array((2 * tokens, columns), F32),
                array((tokens, wide), BF16),
                array((tokens, depth), BF16),
            ),
            in_specs=[VMEM] * 4 + [ANY] + [VMEM] * 2,
            out_specs=(VMEM, VMEM, ANY),
            scratch_shapes=[
                pltpu.VMEM((2, tokens, rows), BF16),
                pltpu.SemaphoreType.DMA((2,)),
            ],
            input_output_aliases={4: 2},
            compiler_params=PARAMS,
            cost_estimate=cost(16 * tokens * cells, 8 * cells),
            name=f"project{hop}",
        )(x, xp, unrotated, total, input_grads, *pieces)

    pairwise = lax.axis_size("rep") == 4
    delta = drift[0]
    if not pairwise:
        base, new_momentum, new_global = outer_plain(delta, momentum, global_weights, master)
    for slot in range(1, line):
        value = arrived[slot][0]
        if slot > 1:
            value = after(value, [sent, repacked] if pairwise and slot == 3 else sent)
        sent = step(slot, 0, value)
        first = lax.ppermute(sent, "fsdp", onward)
        value = arrived[slot][1]
        if pairwise and slot == 1:
            packed, near = outer_pack(after(delta, sent), momentum, global_weights)
        if pairwise and slot == 2:
            repacked, far = outer_repack(after(delta, sent), packed, near)
        waits = [sent, others] if slot == line - 1 else sent
        sent = step(slot, 1, after(value, waits))
        arrived[slot + 1] = (first, lax.ppermute(sent, "fsdp", onward))
        total, other, input_grads = project_hop(
            slot, arrived[slot], after(total, sent), input_grads
        )
        others.append(lax.ppermute(other, "fsdp", swap))
    sum_partner, sum_own = arrived[line]
    sum_swapped = lax.ppermute(after(sum_partner, sent), "fsdp", swap)

    summed = pl.pallas_call(
        functools.partial(early_kernel, line),
        out_shape=array((rows, columns), F32),
        in_specs=[VMEM] * 4,
        out_specs=VMEM,
        compiler_params=PARAMS,
        cost_estimate=cost(0, 0),
        name="early",
    )(x, xp, unrotated, sum_swapped)
    work = 2 * line - 1
    keys, input_grads = pl.pallas_call(
        functools.partial(merge_kernel, line),
        out_shape=(array((tokens, columns), BF16), array((tokens, depth), BF16)),
        in_specs=[VMEM] * 3 + [ANY] * (1 + line),
        out_specs=(VMEM, ANY),
        scratch_shapes=[
            pltpu.VMEM((tokens, columns), BF16),
            pltpu.SemaphoreType.DMA((work,)),
            pltpu.SemaphoreType.DMA,
        ],
        input_output_aliases={3: 1},
        compiler_params=PARAMS,
        cost_estimate=cost(0, 0),
        name="merge",
    )(cosine, sines, after(total, summed), input_grads, *others)
    if pairwise:
        base, new_momentum, new_global = outer_end(
            after(delta, keys), near, far, momentum, global_weights, master
        )
    sum_own = after(sum_own, base)
    merged, first_out, second_out = pl.pallas_call(
        functools.partial(update_kernel, line),
        out_shape=(
            array((rows, columns), F32),
            array((rows, columns), BF16),
            array((rows, columns), BF16),
        ),
        in_specs=[VMEM] * 5,
        out_specs=(ANY,) * 3,
        scratch_shapes=[
            pltpu.VMEM((rows, columns), F32),
            pltpu.VMEM((rows, columns), BF16),
            pltpu.VMEM((rows, columns), BF16),
            pltpu.SemaphoreType.DMA((4, 3)),
        ],
        compiler_params=PARAMS,
        cost_estimate=cost(20 * cells, 18 * cells),
        name="update",
    )(summed, sum_own, first_moment[0], second_moment[0], base)
    return (
        keys[None],
        input_grads[None],
        merged[None],
        first_out[None],
        second_out[None],
        new_momentum,
        new_global,
    )


def solution(mesh):
    sharded = P("rep", "fsdp", None)
    rows = P(("fsdp", "rep"), None)
    return jax.shard_map(
        body,
        mesh=mesh,
        in_specs=(sharded,) * 6 + (rows,) * 2,
        out_specs=(sharded,) * 5 + (rows,) * 2,
        check_vma=False,
    )
```

```python
import functools

import jax
import jax.numpy as jnp
from jax import lax
from jax.experimental import pallas as pl
from jax.experimental.pallas import tpu as pltpu
from jax.sharding import PartitionSpec as P

HEAD = 128
SEQ = 1024

learning_rate = 0.002
beta_one = 0.9
beta_two = 0.95
adam_epsilon = 1e-08
weight_decay = 0.1
outer_rate = 0.7
outer_beta = 0.9
mixing = 0.5
rope_base = 500000.0

VMEM = pl.BlockSpec(memory_space=pltpu.VMEM)
ANY = pl.BlockSpec(memory_space=pl.ANY)
PARAMS = pltpu.CompilerParams(vmem_limit_bytes=10 * 1024 * 1024)
F32 = jnp.float32
BF16 = jnp.bfloat16


def array(shape, kind):
    return jax.ShapeDtypeStruct(shape, kind)


def cost(flops, bytes_accessed):
    return pl.CostEstimate(
        flops=10 * flops, bytes_accessed=10 * bytes_accessed, transcendentals=0
    )


def position(line):
    shard = lax.axis_index("fsdp")
    place, core = lax.div(shard, 2), lax.rem(shard, 2)
    ahead = 1 - 2 * core
    behind = jnp.where(core == 0, place, line - 1 - place)
    return place, core, ahead, behind


def block_at(place, parity, rows):
    return pl.multiple_of((2 * place + parity) * rows, 128)


def rotate_block(values, cosine, sines):
    heads = []
    for at in range(0, values.shape[1], HEAD):
        head = values[:, at : at + HEAD]
        heads.append(head * cosine + pltpu.roll(head, HEAD // 2, 1) * sines)
    return jnp.concatenate(heads, axis=1)


def rope_tables(shard, tokens):
    half_size = HEAD // 2
    token = lax.broadcasted_iota(jnp.int32, (tokens, HEAD), 0)
    column = lax.broadcasted_iota(jnp.int32, (tokens, HEAD), 1)
    exponents = lax.rem(column, half_size).astype(F32) * (2.0 / HEAD)
    inverse_freq = jnp.power(F32(rope_base), -exponents)
    angles = lax.rem(shard * tokens + token, SEQ).astype(F32) * inverse_freq
    sines = jnp.sin(angles)
    return jnp.cos(angles), jnp.where(column < half_size, -sines, sines)


def gradient_term(x, xp, unrotated, at, size):
    columns = pl.ds(at, size)
    left = jnp.concatenate([x[:, columns], xp[:, columns]], axis=0)
    return lax.dot_general(
        left, unrotated[...], (((0,), (0,)), ((), ())), preferred_element_type=F32
    )


def project(x, xp, unrotated, piece, total, stage, other, at, grads, sem):
    columns = pl.ds(at, piece.shape[0])
    tokens = x.shape[0]
    both = jnp.concatenate([x[:, columns], xp[:, columns]], axis=0)
    total[...] += jnp.dot(both, piece[...], preferred_element_type=F32)
    made = lax.dot_general(
        unrotated[...], piece[...], (((1,), (1,)), ((), ())), preferred_element_type=F32
    ).astype(BF16)
    stage[...] = made[:tokens, :]
    other[...] = made[tokens:, :]
    pltpu.make_async_copy(stage, grads.at[:, columns], sem).start()


def project_wait(stage, grads, at, sem):
    pltpu.make_async_copy(stage, grads.at[:, pl.ds(at, stage.shape[1])], sem).wait()


def local_kernel(line, x, xp, kg, kgp, low, *refs):
    unrotated, cosine, sines, total, other, grads, stage, sem = refs
    tokens = x.shape[0]
    place, core, _, _ = position(line)
    shard = 2 * place + core
    for half, source in enumerate((kg, kgp)):
        cosines, signed = rope_tables(jnp.bitwise_xor(shard, half), tokens)
        unrotated[half * tokens : (half + 1) * tokens, :] = rotate_block(
            source[...].astype(F32), cosines, -signed
        ).astype(BF16)
        if half == 0:
            cosine[...] = cosines
            sines[...] = signed
    total[...] = jnp.zeros_like(total)
    at = block_at(place, core, low.shape[0])
    project(x, xp, unrotated, low, total, stage, other, at, grads, sem)
    project_wait(stage, grads, at, sem)


def project_kernel(line, hop, x, xp, unrotated, total_in, grads_in, *refs):
    del grads_in
    first, second, total, other, grads, stage, sems = refs
    tokens = x.shape[0]
    rows = first.shape[0]
    place, core, ahead, behind = position(line)
    total[...] = total_in[...]

    @pl.when(behind >= hop)
    def _():
        work = [(first, core), (second, 1 - core)]
        ats = [block_at(place - hop * ahead, parity, rows) for _, parity in work]
        for i, (piece, _) in enumerate(work):
            into = other.at[:, i * rows : (i + 1) * rows]
            project(
                x, xp, unrotated, piece, total, stage.at[i], into, ats[i], grads, sems.at[i]
            )
        for i in range(2):
            project_wait(stage.at[i], grads, ats[i], sems.at[i])

    if hop == line - 1:
        other[:, 2 * rows :] = total[tokens:, :].astype(BF16)


def merge_kernel(line, cosine, sines, total, grads_in, *refs):
    del grads_in
    others = refs[:line]
    keys, grads, partial, sems, sem = refs[line:]
    tokens, _ = keys.shape
    rows = others[0].shape[1]
    place, core, ahead, behind = position(line)
    work = [(behind >= 0, place, 1 - core, others[0].at[:, :])]
    for hop in range(1, line):
        for i, parity in enumerate((1 - core, core)):
            part = others[hop].at[:, i * rows : (i + 1) * rows]
            work.append((behind + hop < line, place + hop * ahead, parity, part))

    def copy(i):
        _, owner, parity, part = work[i]
        at = pl.ds(block_at(owner, parity, rows), rows)
        return pltpu.make_async_copy(part, grads.at[:, at], sems.at[i])

    rest = pltpu.make_async_copy(others[line - 1].at[:, 2 * rows :], partial, sem)
    rest.start()
    for i in range(len(work)):
        pl.when(work[i][0])(lambda i=i: copy(i).start())
    rest.wait()
    keys[...] = rotate_block(
        total[:tokens, :] + partial[...].astype(F32), cosine[...], sines[...]
    ).astype(BF16)
    for i in range(len(work)):
        pl.when(work[i][0])(lambda i=i: copy(i).wait())


def step_kernel(line, slot, half, arrived, x, xp, unrotated, sent):
    place, core, ahead, behind = position(line)
    rows = arrived.shape[0]
    size = min(rows, 256)
    parity = core if half else 1 - core

    @pl.when(behind >= slot)
    def _():
        sent[...] = arrived[...]

    @pl.when(behind < slot)
    def _():
        owner = place + (line - slot) * ahead
        for at in range(0, rows, size):
            term = gradient_term(
                x, xp, unrotated, pl.multiple_of(block_at(owner, parity, rows) + at, 128), size
            )
            before = arrived[at : at + size, :].astype(F32)
            sent[at : at + size, :] = (term + jnp.where(behind > 0, before, 0.0)).astype(BF16)


def split_kernel(whole, *parts):
    size = parts[0].shape[0]
    for i, part in enumerate(parts):
        part[...] = whole[i * size : (i + 1) * size, :]


def early_kernel(line, x, xp, unrotated, *refs):
    *parts, summed = refs
    place, core, _, behind = position(line)
    rows = summed.shape[0]
    size = parts[0].shape[0]
    for i, part in enumerate(parts):
        at = i * size
        term = gradient_term(
            x, xp, unrotated, pl.multiple_of(block_at(place, core, rows) + at, 128), size
        )
        other = part[...].astype(F32)
        summed[at : at + size, :] = term + jnp.where(behind < line - 1, other, 0.0)


def update_kernel(line, summed, arrived, first, second, base, merged, first_out, second_out, *scratch):
    merged_v, first_v, second_v, sem = scratch
    behind = position(line)[3]
    rows = summed.shape[0]
    parts = 4
    size = rows // parts
    chunk = min(size, 32)
    outs = ((merged_v, merged), (first_v, first_out), (second_v, second_out))

    def copies(part):
        at = pl.ds(part * size, size)
        return [
            pltpu.make_async_copy(source.at[at, :], target.at[at, :], sem.at[part, i])
            for i, (source, target) in enumerate(outs)
        ]

    for part in range(parts):

        def some(i, carry, part=part):
            at = pl.ds(pl.multiple_of(part * size + i * chunk, 16), chunk)
            gradient = summed[at, :] + jnp.where(behind > 0, arrived[at, :].astype(F32), 0.0)
            one = beta_one * first[at, :].astype(F32) + (1.0 - beta_one) * gradient
            two = beta_two * second[at, :].astype(F32) + (1.0 - beta_two) * gradient * gradient
            inverse = lax.rsqrt(two)
            step = one * (inverse * (2.0 - (two * inverse + adam_epsilon) * inverse))
            merged_v[at, :] = base[at, :] - (mixing * learning_rate) * step
            first_v[at, :] = one.astype(BF16)
            second_v[at, :] = two.astype(BF16)
            return carry

        lax.fori_loop(0, size // chunk, some, 0, unroll=True)
        for copy in copies(part):
            copy.start()
    for part in range(parts):
        for copy in copies(part):
            copy.wait()


outer_held = outer_rate * outer_beta * outer_beta
outer_slope = outer_rate * (1.0 + outer_beta)


def pack_kernel(drift, momentum, global_weights, packed):
    rows = drift.shape[0]
    packed[:rows, :] = drift[...].astype(BF16)
    packed[rows:, :] = (global_weights[...] - outer_held * momentum[...]).astype(BF16)


def repack_kernel(drift, mine, other, packed):
    rows = drift.shape[0]
    size = mine.shape[0] - rows
    packed[:rows, :] = (drift[...] + other[:rows, :].astype(F32)).astype(BF16)
    packed[rows : rows + size, :] = mine[rows:, :]
    packed[rows + size :, :] = other[rows:, :]


def outer_kernel(drift, near, far, momentum, global_weights, weights, *refs):
    base, new_momentum, new_global = refs
    rows = drift.shape[0]
    size = momentum.shape[0]
    replica = lax.axis_index("rep")
    core = lax.rem(lax.axis_index("fsdp"), 2)
    held = (None, near.at[rows:, :], far.at[rows : rows + size, :], far.at[rows + size :, :])
    for shift, other in enumerate((0, 1 + core, 2 - core, 3)):
        at = pl.ds(pl.multiple_of(jnp.bitwise_xor(replica, other) * size, size), size)
        total = drift[at, :] + near[at, :].astype(F32) + far[at, :].astype(F32)
        mean_drift = total / 4
        if shift == 0:
            moment = outer_beta * momentum[...] + mean_drift
            updated = global_weights[...] - outer_rate * (mean_drift + outer_beta * moment)
            new_momentum[...] = moment
            new_global[...] = updated
        else:
            updated = held[shift][...].astype(F32) - outer_slope * mean_drift
        base[at, :] = (mixing * (1.0 - learning_rate * weight_decay)) * weights[at, :] + (
            1.0 - mixing
        ) * updated


def pairs_of(turn, shards):
    return [
        (i * shards + j, (i ^ (1 + (j + turn) % 2)) * shards + j)
        for i in range(4)
        for j in range(shards)
    ]


def outer_pack(drift, momentum, global_weights):
    rows, columns = drift.shape
    packed = pl.pallas_call(
        pack_kernel,
        out_shape=array((rows + momentum.shape[0], columns), BF16),
        in_specs=[VMEM] * 3,
        out_specs=VMEM,
        compiler_params=PARAMS,
        cost_estimate=cost(0, 0),
        name="pack",
    )(drift, momentum, global_weights)
    near = lax.ppermute(packed, ("rep", "fsdp"), pairs_of(0, lax.axis_size("fsdp")))
    return packed, near


def outer_repack(drift, packed, near):
    rows, columns = drift.shape
    repacked = pl.pallas_call(
        repack_kernel,
        out_shape=array((2 * packed.shape[0] - rows, columns), BF16),
        in_specs=[VMEM] * 3,
        out_specs=VMEM,
        compiler_params=PARAMS,
        cost_estimate=cost(0, 0),
        name="repack",
    )(drift, packed, near)
    return repacked, lax.ppermute(repacked, ("rep", "fsdp"), pairs_of(1, lax.axis_size("fsdp")))


def outer_end(drift, near, far, momentum, global_weights, weights):
    rows, columns = drift.shape
    size = momentum.shape[0]
    return pl.pallas_call(
        outer_kernel,
        out_shape=(
            array((rows, columns), F32),
            array((size, columns), F32),
            array((size, columns), F32),
        ),
        in_specs=[VMEM] * 6,
        out_specs=(VMEM,) * 3,
        compiler_params=PARAMS,
        cost_estimate=cost(0, 0),
        name="outer",
    )(drift, near, far, momentum, global_weights, weights)


def outer_plain(drift, momentum, global_weights, weights):
    replicas = lax.axis_size("rep")
    size = momentum.shape[0]
    mean_drift = lax.psum(drift, "rep") / replicas
    whole = [lax.all_gather(a, "rep", axis=0, tiled=True) for a in (momentum, global_weights)]
    moment = outer_beta * whole[0] + mean_drift
    updated = whole[1] - outer_rate * (mean_drift + outer_beta * moment)
    base = (mixing * (1.0 - learning_rate * weight_decay)) * weights + (1.0 - mixing) * updated
    at = lax.axis_index("rep") * size
    return (
        base,
        lax.dynamic_slice_in_dim(moment, at, size, 0),
        lax.dynamic_slice_in_dim(updated, at, size, 0),
    )


def after(first, then):
    return lax.optimization_barrier((first, then))[0]


def body(inputs, key_grads, weights, first_moment, second_moment, drift, momentum, global_weights):
    x, kg, master = inputs[0], key_grads[0], weights[0]
    tokens, depth = x.shape
    rows, columns = master.shape
    shards = lax.axis_size("fsdp")
    line = shards // 2
    swap = [(i, i ^ 1) for i in range(shards)]
    onward = [(i, i + 2) for i in range(0, shards - 2, 2)] + [(shards - 2, shards - 1)]
    onward += [(i, i - 2) for i in range(3, shards, 2)] + [(1, 0)]
    piece = array((rows, columns), BF16)
    cells = rows * columns
    summed_cost = cost(4 * tokens * cells, 6 * cells + 4 * tokens * rows)

    low = master.astype(BF16)
    first_a = lax.ppermute(low, "fsdp", onward)
    low_partner = lax.ppermute(low, "fsdp", swap)
    arrived = {1: (first_a, lax.ppermute(low_partner, "fsdp", onward))}
    xp = lax.ppermute(x, "fsdp", swap)
    kgp = lax.ppermute(kg, "fsdp", swap)

    unrotated, cosine, sines, total, other, input_grads = pl.pallas_call(
        functools.partial(local_kernel, line),
        out_shape=(
            array((2 * tokens, columns), BF16),
            array((tokens, HEAD), F32),
            array((tokens, HEAD), F32),
            array((2 * tokens, columns), F32),
            array((tokens, rows), BF16),
            array((tokens, depth), BF16),
        ),
        in_specs=[VMEM] * 5,
        out_specs=(VMEM,) * 5 + (ANY,),
        scratch_shapes=[pltpu.VMEM((tokens, rows), BF16), pltpu.SemaphoreType.DMA],
        compiler_params=PARAMS,
        cost_estimate=cost(8 * tokens * cells, 6 * cells),
        name="local",
    )(x, xp, kg, kgp, low)

    def step(slot, half, value):
        return pl.pallas_call(
            functools.partial(step_kernel, line, slot, half),
            out_shape=piece,
            in_specs=[VMEM] * 4,
            out_specs=VMEM,
            compiler_params=PARAMS,
            cost_estimate=summed_cost,
            name=f"step{slot}{'ab'[half]}",
        )(value, x, xp, unrotated)

    others = [lax.ppermute(other, "fsdp", swap)]

    def project_hop(hop, pieces, total, input_grads):
        wide = 2 * rows + (columns if hop == line - 1 else 0)
        return pl.pallas_call(
            functools.partial(project_kernel, line, hop),
            out_shape=(
                array((2 * tokens, columns), F32),
                array((tokens, wide), BF16),
                array((tokens, depth), BF16),
            ),
            in_specs=[VMEM] * 4 + [ANY] + [VMEM] * 2,
            out_specs=(VMEM, VMEM, ANY),
            scratch_shapes=[
                pltpu.VMEM((2, tokens, rows), BF16),
                pltpu.SemaphoreType.DMA((2,)),
            ],
            input_output_aliases={4: 2},
            compiler_params=PARAMS,
            cost_estimate=cost(0, 0) if hop == line - 1 else cost(16 * tokens * cells, 8 * cells),
            name=f"project{hop}",
        )(x, xp, unrotated, total, input_grads, *pieces)

    pairwise = lax.axis_size("rep") == 4
    delta = drift[0]
    if not pairwise:
        base, new_momentum, new_global = outer_plain(delta, momentum, global_weights, master)
    for slot in range(1, line):
        value = arrived[slot][0]
        if slot > 1:
            value = after(value, [sent, repacked] if pairwise and slot == 3 else sent)
        sent = step(slot, 0, value)
        first = lax.ppermute(sent, "fsdp", onward)
        value = arrived[slot][1]
        if pairwise and slot == 1:
            packed, near = outer_pack(after(delta, sent), momentum, global_weights)
        if pairwise and slot == 2:
            repacked, far = outer_repack(after(delta, sent), packed, near)
        waits = [sent, others] if slot == line - 1 else sent
        sent = step(slot, 1, after(value, waits))
        arrived[slot + 1] = (first, lax.ppermute(sent, "fsdp", onward))
        total, other, input_grads = project_hop(
            slot, arrived[slot], after(total, sent), input_grads
        )
        others.append(lax.ppermute(other, "fsdp", swap))
    sum_partner, sum_own = arrived[line]
    sums = pl.pallas_call(
        split_kernel,
        out_shape=(array((rows // 2, columns), BF16),) * 2,
        in_specs=[VMEM],
        out_specs=(VMEM, VMEM),
        compiler_params=PARAMS,
        cost_estimate=cost(0, 0),
        name="split",
    )(after(sum_partner, [sent, total]))
    sums_swapped = [lax.ppermute(part, "fsdp", swap) for part in sums]

    summed = pl.pallas_call(
        functools.partial(early_kernel, line),
        out_shape=array((rows, columns), F32),
        in_specs=[VMEM] * 5,
        out_specs=VMEM,
        compiler_params=PARAMS,
        cost_estimate=cost(0, 0),
        name="early",
    )(x, xp, unrotated, *sums_swapped)
    work = 2 * line - 1
    keys, input_grads = pl.pallas_call(
        functools.partial(merge_kernel, line),
        out_shape=(array((tokens, columns), BF16), array((tokens, depth), BF16)),
        in_specs=[VMEM] * 3 + [ANY] * (1 + line),
        out_specs=(VMEM, ANY),
        scratch_shapes=[
            pltpu.VMEM((tokens, columns), BF16),
            pltpu.SemaphoreType.DMA((work,)),
            pltpu.SemaphoreType.DMA,
        ],
        input_output_aliases={3: 1},
        compiler_params=PARAMS,
        cost_estimate=cost(0, 0),
        name="merge",
    )(cosine, sines, after(total, summed), input_grads, *others)
    if pairwise:
        base, new_momentum, new_global = outer_end(
            after(delta, keys), near, far, momentum, global_weights, master
        )
    sum_own = after(sum_own, base)
    merged, first_out, second_out = pl.pallas_call(
        functools.partial(update_kernel, line),
        out_shape=(
            array((rows, columns), F32),
            array((rows, columns), BF16),
            array((rows, columns), BF16),
        ),
        in_specs=[VMEM] * 5,
        out_specs=(ANY,) * 3,
        scratch_shapes=[
            pltpu.VMEM((rows, columns), F32),
            pltpu.VMEM((rows, columns), BF16),
            pltpu.VMEM((rows, columns), BF16),
            pltpu.SemaphoreType.DMA((4, 3)),
        ],
        compiler_params=PARAMS,
        cost_estimate=cost(20 * cells, 18 * cells),
        name="update",
    )(summed, sum_own, first_moment[0], second_moment[0], base)
    return (
        keys[None],
        input_grads[None],
        merged[None],
        first_out[None],
        second_out[None],
        new_momentum,
        new_global,
    )


def solution(mesh):
    sharded = P("rep", "fsdp", None)
    rows = P(("fsdp", "rep"), None)
    return jax.shard_map(
        body,
        mesh=mesh,
        in_specs=(sharded,) * 6 + (rows,) * 2,
        out_specs=(sharded,) * 5 + (rows,) * 2,
        check_vma=False,
    )
```

```python
import functools

import jax
import jax.numpy as jnp
from jax import lax
from jax.experimental import pallas as pl
from jax.experimental.pallas import tpu as pltpu
from jax.sharding import PartitionSpec as P

HEAD = 128
SEQ = 1024

learning_rate = 0.002
beta_one = 0.9
beta_two = 0.95
adam_epsilon = 1e-08
weight_decay = 0.1
outer_rate = 0.7
outer_beta = 0.9
mixing = 0.5
rope_base = 500000.0

VMEM = pl.BlockSpec(memory_space=pltpu.VMEM)
ANY = pl.BlockSpec(memory_space=pl.ANY)
PARAMS = pltpu.CompilerParams(vmem_limit_bytes=10 * 1024 * 1024)
F32 = jnp.float32
BF16 = jnp.bfloat16


def array(shape, kind):
    return jax.ShapeDtypeStruct(shape, kind)


def cost(flops, bytes_accessed):
    return pl.CostEstimate(
        flops=10 * flops, bytes_accessed=10 * bytes_accessed, transcendentals=0
    )


def position(line):
    shard = lax.axis_index("fsdp")
    place, core = lax.div(shard, 2), lax.rem(shard, 2)
    ahead = 1 - 2 * core
    behind = jnp.where(core == 0, place, line - 1 - place)
    return place, core, ahead, behind


def block_at(place, parity, rows):
    return pl.multiple_of((2 * place + parity) * rows, 128)


def rotate_block(values, cosine, sines):
    heads = []
    for at in range(0, values.shape[1], HEAD):
        head = values[:, at : at + HEAD]
        heads.append(head * cosine + pltpu.roll(head, HEAD // 2, 1) * sines)
    return jnp.concatenate(heads, axis=1)


def rope_tables(shard, tokens):
    half_size = HEAD // 2
    token = lax.broadcasted_iota(jnp.int32, (tokens, HEAD), 0)
    column = lax.broadcasted_iota(jnp.int32, (tokens, HEAD), 1)
    exponents = lax.rem(column, half_size).astype(F32) * (2.0 / HEAD)
    inverse_freq = jnp.power(F32(rope_base), -exponents)
    angles = lax.rem(shard * tokens + token, SEQ).astype(F32) * inverse_freq
    sines = jnp.sin(angles)
    return jnp.cos(angles), jnp.where(column < half_size, -sines, sines)


def gradient_term(x, xp, unrotated, at, size):
    columns = pl.ds(at, size)
    left = jnp.concatenate([x[:, columns], xp[:, columns]], axis=0)
    return lax.dot_general(
        left, unrotated[...], (((0,), (0,)), ((), ())), preferred_element_type=F32
    )


def project(x, xp, unrotated, piece, total, stage, other, at, grads, sem):
    columns = pl.ds(at, piece.shape[0])
    tokens = x.shape[0]
    both = jnp.concatenate([x[:, columns], xp[:, columns]], axis=0)
    total[...] += jnp.dot(both, piece[...], preferred_element_type=F32)
    made = lax.dot_general(
        unrotated[...], piece[...], (((1,), (1,)), ((), ())), preferred_element_type=F32
    ).astype(BF16)
    stage[...] = made[:tokens, :]
    other[...] = made[tokens:, :]
    pltpu.make_async_copy(stage, grads.at[:, columns], sem).start()


def project_wait(stage, grads, at, sem):
    pltpu.make_async_copy(stage, grads.at[:, pl.ds(at, stage.shape[1])], sem).wait()


def local_kernel(line, x, xp, kg, kgp, low, *refs):
    unrotated, cosine, sines, total, other, grads, stage, sem = refs
    tokens = x.shape[0]
    place, core, _, _ = position(line)
    shard = 2 * place + core
    for half, source in enumerate((kg, kgp)):
        cosines, signed = rope_tables(jnp.bitwise_xor(shard, half), tokens)
        unrotated[half * tokens : (half + 1) * tokens, :] = rotate_block(
            source[...].astype(F32), cosines, -signed
        ).astype(BF16)
        if half == 0:
            cosine[...] = cosines
            sines[...] = signed
    total[...] = jnp.zeros_like(total)
    at = block_at(place, core, low.shape[0])
    project(x, xp, unrotated, low, total, stage, other, at, grads, sem)
    project_wait(stage, grads, at, sem)


def project_kernel(line, hop, x, xp, unrotated, total_in, grads_in, *refs):
    del grads_in
    first, second, total, other, grads, stage, sems = refs
    tokens = x.shape[0]
    rows = first.shape[0]
    place, core, ahead, behind = position(line)
    total[...] = total_in[...]

    @pl.when(behind >= hop)
    def _():
        work = [(first, core), (second, 1 - core)]
        ats = [block_at(place - hop * ahead, parity, rows) for _, parity in work]
        for i, (piece, _) in enumerate(work):
            into = other.at[:, i * rows : (i + 1) * rows]
            project(
                x, xp, unrotated, piece, total, stage.at[i], into, ats[i], grads, sems.at[i]
            )
        for i in range(2):
            project_wait(stage.at[i], grads, ats[i], sems.at[i])

    if hop == line - 1:
        other[:, 2 * rows :] = total[tokens:, :].astype(BF16)


def merge_kernel(line, cosine, sines, total, grads_in, *refs):
    del grads_in
    others = refs[:line]
    keys, grads, partial, sems, sem = refs[line:]
    tokens, _ = keys.shape
    rows = others[0].shape[1]
    place, core, ahead, behind = position(line)
    work = [(behind >= 0, place, 1 - core, others[0].at[:, :])]
    for hop in range(1, line):
        for i, parity in enumerate((1 - core, core)):
            part = others[hop].at[:, i * rows : (i + 1) * rows]
            work.append((behind + hop < line, place + hop * ahead, parity, part))

    def copy(i):
        _, owner, parity, part = work[i]
        at = pl.ds(block_at(owner, parity, rows), rows)
        return pltpu.make_async_copy(part, grads.at[:, at], sems.at[i])

    rest = pltpu.make_async_copy(others[line - 1].at[:, 2 * rows :], partial, sem)
    rest.start()
    for i in range(len(work)):
        pl.when(work[i][0])(lambda i=i: copy(i).start())
    rest.wait()
    keys[...] = rotate_block(
        total[:tokens, :] + partial[...].astype(F32), cosine[...], sines[...]
    ).astype(BF16)
    for i in range(len(work)):
        pl.when(work[i][0])(lambda i=i: copy(i).wait())


def step_kernel(line, slot, half, arrived, x, xp, unrotated, sent):
    place, core, ahead, behind = position(line)
    rows = arrived.shape[0]
    size = min(rows, 256)
    parity = core if half else 1 - core

    @pl.when(behind >= slot)
    def _():
        sent[...] = arrived[...]

    @pl.when(behind < slot)
    def _():
        owner = place + (line - slot) * ahead
        for at in range(0, rows, size):
            term = gradient_term(
                x, xp, unrotated, pl.multiple_of(block_at(owner, parity, rows) + at, 128), size
            )
            before = arrived[at : at + size, :].astype(F32)
            sent[at : at + size, :] = (term + jnp.where(behind > 0, before, 0.0)).astype(BF16)


def scale_kernel(first, second, first_scaled, second_scaled):
    first_scaled[...] = beta_one * first[...].astype(F32)
    second_scaled[...] = beta_two * second[...].astype(F32)


def split_kernel(whole, *parts):
    size = parts[0].shape[0]
    for i, part in enumerate(parts):
        part[...] = whole[i * size : (i + 1) * size, :]


def early_kernel(line, x, xp, unrotated, *refs):
    *parts, summed = refs
    place, core, _, behind = position(line)
    rows = summed.shape[0]
    size = parts[0].shape[0]
    for i, part in enumerate(parts):
        at = i * size
        term = gradient_term(
            x, xp, unrotated, pl.multiple_of(block_at(place, core, rows) + at, 128), size
        )
        other = part[...].astype(F32)
        summed[at : at + size, :] = term + jnp.where(behind < line - 1, other, 0.0)


def update_kernel(line, summed, arrived, first, second, base, merged, first_out, second_out, *scratch):
    merged_v, first_v, second_v, sem = scratch
    behind = position(line)[3]
    rows = summed.shape[0]
    parts = sem.shape[0]
    size = rows // parts
    chunk = min(size, 32)
    outs = ((merged_v, merged), (first_v, first_out), (second_v, second_out))

    def copies(part):
        at = pl.ds(part * size, size)
        return [
            pltpu.make_async_copy(source.at[at, :], target.at[at, :], sem.at[part, i])
            for i, (source, target) in enumerate(outs)
        ]

    for part in range(parts):

        def some(i, carry, part=part):
            at = pl.ds(pl.multiple_of(part * size + i * chunk, 16), chunk)
            gradient = summed[at, :] + jnp.where(behind > 0, arrived[at, :].astype(F32), 0.0)
            one = first[at, :] + (1.0 - beta_one) * gradient
            two = second[at, :] + (1.0 - beta_two) * gradient * gradient
            inverse = lax.rsqrt(two)
            step = one * (inverse * (2.0 - (two * inverse + adam_epsilon) * inverse))
            merged_v[at, :] = base[at, :] - (mixing * learning_rate) * step
            first_v[at, :] = one.astype(BF16)
            second_v[at, :] = two.astype(BF16)
            return carry

        lax.fori_loop(0, size // chunk, some, 0, unroll=True)
        for copy in copies(part):
            copy.start()
    for part in range(parts):
        for copy in copies(part):
            copy.wait()


outer_held = outer_rate * outer_beta * outer_beta
outer_slope = outer_rate * (1.0 + outer_beta)


def pack_kernel(drift, momentum, global_weights, packed):
    rows = drift.shape[0]
    packed[:rows, :] = drift[...].astype(BF16)
    packed[rows:, :] = (global_weights[...] - outer_held * momentum[...]).astype(BF16)


def repack_kernel(drift, mine, other, packed):
    rows = drift.shape[0]
    size = mine.shape[0] - rows
    packed[:rows, :] = (drift[...] + other[:rows, :].astype(F32)).astype(BF16)
    packed[rows : rows + size, :] = mine[rows:, :]
    packed[rows + size :, :] = other[rows:, :]


def outer_kernel(drift, near, far, momentum, global_weights, weights, *refs):
    base, new_momentum, new_global = refs
    rows = drift.shape[0]
    size = momentum.shape[0]
    replica = lax.axis_index("rep")
    core = lax.rem(lax.axis_index("fsdp"), 2)
    held = (None, near.at[rows:, :], far.at[rows : rows + size, :], far.at[rows + size :, :])
    for shift, other in enumerate((0, 1 + core, 2 - core, 3)):
        at = pl.ds(pl.multiple_of(jnp.bitwise_xor(replica, other) * size, size), size)
        total = drift[at, :] + near[at, :].astype(F32) + far[at, :].astype(F32)
        mean_drift = total / 4
        if shift == 0:
            moment = outer_beta * momentum[...] + mean_drift
            updated = global_weights[...] - outer_rate * (mean_drift + outer_beta * moment)
            new_momentum[...] = moment
            new_global[...] = updated
        else:
            updated = held[shift][...].astype(F32) - outer_slope * mean_drift
        base[at, :] = (mixing * (1.0 - learning_rate * weight_decay)) * weights[at, :] + (
            1.0 - mixing
        ) * updated


def pairs_of(turn, shards):
    return [
        (i * shards + j, (i ^ (1 + (j + turn) % 2)) * shards + j)
        for i in range(4)
        for j in range(shards)
    ]


def outer_pack(drift, momentum, global_weights):
    rows, columns = drift.shape
    packed = pl.pallas_call(
        pack_kernel,
        out_shape=array((rows + momentum.shape[0], columns), BF16),
        in_specs=[VMEM] * 3,
        out_specs=VMEM,
        compiler_params=PARAMS,
        cost_estimate=cost(0, 0),
        name="pack",
    )(drift, momentum, global_weights)
    near = lax.ppermute(packed, ("rep", "fsdp"), pairs_of(0, lax.axis_size("fsdp")))
    return packed, near


def outer_repack(drift, packed, near):
    rows, columns = drift.shape
    repacked = pl.pallas_call(
        repack_kernel,
        out_shape=array((2 * packed.shape[0] - rows, columns), BF16),
        in_specs=[VMEM] * 3,
        out_specs=VMEM,
        compiler_params=PARAMS,
        cost_estimate=cost(0, 0),
        name="repack",
    )(drift, packed, near)
    return repacked, lax.ppermute(repacked, ("rep", "fsdp"), pairs_of(1, lax.axis_size("fsdp")))


def outer_end(drift, near, far, momentum, global_weights, weights):
    rows, columns = drift.shape
    size = momentum.shape[0]
    return pl.pallas_call(
        outer_kernel,
        out_shape=(
            array((rows, columns), F32),
            array((size, columns), F32),
            array((size, columns), F32),
        ),
        in_specs=[VMEM] * 6,
        out_specs=(VMEM,) * 3,
        compiler_params=PARAMS,
        cost_estimate=cost(0, 0),
        name="outer",
    )(drift, near, far, momentum, global_weights, weights)


def outer_plain(drift, momentum, global_weights, weights):
    replicas = lax.axis_size("rep")
    size = momentum.shape[0]
    mean_drift = lax.psum(drift, "rep") / replicas
    whole = [lax.all_gather(a, "rep", axis=0, tiled=True) for a in (momentum, global_weights)]
    moment = outer_beta * whole[0] + mean_drift
    updated = whole[1] - outer_rate * (mean_drift + outer_beta * moment)
    base = (mixing * (1.0 - learning_rate * weight_decay)) * weights + (1.0 - mixing) * updated
    at = lax.axis_index("rep") * size
    return (
        base,
        lax.dynamic_slice_in_dim(moment, at, size, 0),
        lax.dynamic_slice_in_dim(updated, at, size, 0),
    )


def after(first, then):
    return lax.optimization_barrier((first, then))[0]


def body(inputs, key_grads, weights, first_moment, second_moment, drift, momentum, global_weights):
    x, kg, master = inputs[0], key_grads[0], weights[0]
    tokens, depth = x.shape
    rows, columns = master.shape
    shards = lax.axis_size("fsdp")
    line = shards // 2
    swap = [(i, i ^ 1) for i in range(shards)]
    onward = [(i, i + 2) for i in range(0, shards - 2, 2)] + [(shards - 2, shards - 1)]
    onward += [(i, i - 2) for i in range(3, shards, 2)] + [(1, 0)]
    piece = array((rows, columns), BF16)
    cells = rows * columns
    summed_cost = cost(4 * tokens * cells, 6 * cells + 4 * tokens * rows)

    low = master.astype(BF16)
    first_a = lax.ppermute(low, "fsdp", onward)
    low_partner = lax.ppermute(low, "fsdp", swap)
    arrived = {1: (first_a, lax.ppermute(low_partner, "fsdp", onward))}
    xp = lax.ppermute(x, "fsdp", swap)
    kgp = lax.ppermute(kg, "fsdp", swap)

    unrotated, cosine, sines, total, other, input_grads = pl.pallas_call(
        functools.partial(local_kernel, line),
        out_shape=(
            array((2 * tokens, columns), BF16),
            array((tokens, HEAD), F32),
            array((tokens, HEAD), F32),
            array((2 * tokens, columns), F32),
            array((tokens, rows), BF16),
            array((tokens, depth), BF16),
        ),
        in_specs=[VMEM] * 5,
        out_specs=(VMEM,) * 5 + (ANY,),
        scratch_shapes=[pltpu.VMEM((tokens, rows), BF16), pltpu.SemaphoreType.DMA],
        compiler_params=PARAMS,
        cost_estimate=cost(8 * tokens * cells, 6 * cells),
        name="local",
    )(x, xp, kg, kgp, low)

    def step(slot, half, value):
        return pl.pallas_call(
            functools.partial(step_kernel, line, slot, half),
            out_shape=piece,
            in_specs=[VMEM] * 4,
            out_specs=VMEM,
            compiler_params=PARAMS,
            cost_estimate=summed_cost,
            name=f"step{slot}{'ab'[half]}",
        )(value, x, xp, unrotated)

    others = [lax.ppermute(other, "fsdp", swap)]

    def project_hop(hop, pieces, total, input_grads):
        wide = 2 * rows + (columns if hop == line - 1 else 0)
        return pl.pallas_call(
            functools.partial(project_kernel, line, hop),
            out_shape=(
                array((2 * tokens, columns), F32),
                array((tokens, wide), BF16),
                array((tokens, depth), BF16),
            ),
            in_specs=[VMEM] * 4 + [ANY] + [VMEM] * 2,
            out_specs=(VMEM, VMEM, ANY),
            scratch_shapes=[
                pltpu.VMEM((2, tokens, rows), BF16),
                pltpu.SemaphoreType.DMA((2,)),
            ],
            input_output_aliases={4: 2},
            compiler_params=PARAMS,
            cost_estimate=cost(0, 0) if hop == line - 1 else cost(16 * tokens * cells, 8 * cells),
            name=f"project{hop}",
        )(x, xp, unrotated, total, input_grads, *pieces)

    pairwise = lax.axis_size("rep") == 4
    delta = drift[0]
    if not pairwise:
        base, new_momentum, new_global = outer_plain(delta, momentum, global_weights, master)
    for slot in range(1, line):
        value = arrived[slot][0]
        if slot > 1:
            value = after(value, [sent, repacked] if pairwise and slot == 3 else sent)
        sent = step(slot, 0, value)
        first = lax.ppermute(sent, "fsdp", onward)
        value = arrived[slot][1]
        if pairwise and slot == 1:
            packed, near = outer_pack(after(delta, sent), momentum, global_weights)
        if pairwise and slot == 2:
            repacked, far = outer_repack(after(delta, sent), packed, near)
        waits = [sent, others] if slot == line - 1 else sent
        sent = step(slot, 1, after(value, waits))
        arrived[slot + 1] = (first, lax.ppermute(sent, "fsdp", onward))
        total, other, input_grads = project_hop(
            slot, arrived[slot], after(total, sent), input_grads
        )
        others.append(lax.ppermute(other, "fsdp", swap))
    sum_partner, sum_own = arrived[line]
    scaled = pl.pallas_call(
        scale_kernel,
        out_shape=(array((rows, columns), F32),) * 2,
        in_specs=[VMEM, VMEM],
        out_specs=(VMEM, VMEM),
        compiler_params=PARAMS,
        cost_estimate=cost(0, 0),
        name="scale",
    )(after(first_moment[0], sent), second_moment[0])
    sums = pl.pallas_call(
        split_kernel,
        out_shape=(array((rows // 2, columns), BF16),) * 2,
        in_specs=[VMEM],
        out_specs=(VMEM, VMEM),
        compiler_params=PARAMS,
        cost_estimate=cost(0, 0),
        name="split",
    )(after(sum_partner, [total, scaled]))
    sums_swapped = [lax.ppermute(part, "fsdp", swap) for part in sums]

    work = 2 * line - 1
    keys, input_grads = pl.pallas_call(
        functools.partial(merge_kernel, line),
        out_shape=(array((tokens, columns), BF16), array((tokens, depth), BF16)),
        in_specs=[VMEM] * 3 + [ANY] * (1 + line),
        out_specs=(VMEM, ANY),
        scratch_shapes=[
            pltpu.VMEM((tokens, columns), BF16),
            pltpu.SemaphoreType.DMA((work,)),
            pltpu.SemaphoreType.DMA,
        ],
        input_output_aliases={3: 1},
        compiler_params=PARAMS,
        cost_estimate=cost(0, 0),
        name="merge",
    )(cosine, sines, total, input_grads, *others)
    summed = pl.pallas_call(
        functools.partial(early_kernel, line),
        out_shape=array((rows, columns), F32),
        in_specs=[VMEM] * 5,
        out_specs=VMEM,
        compiler_params=PARAMS,
        cost_estimate=cost(0, 0),
        name="early",
    )(x, xp, after(unrotated, keys), *sums_swapped)
    if pairwise:
        base, new_momentum, new_global = outer_end(
            after(delta, summed), near, far, momentum, global_weights, master
        )
    sum_own = after(sum_own, base)
    update_parts = 8 if rows % 256 == 0 else 1
    merged, first_out, second_out = pl.pallas_call(
        functools.partial(update_kernel, line),
        out_shape=(
            array((rows, columns), F32),
            array((rows, columns), BF16),
            array((rows, columns), BF16),
        ),
        in_specs=[VMEM] * 5,
        out_specs=(ANY,) * 3,
        scratch_shapes=[
            pltpu.VMEM((rows, columns), F32),
            pltpu.VMEM((rows, columns), BF16),
            pltpu.VMEM((rows, columns), BF16),
            pltpu.SemaphoreType.DMA((update_parts, 3)),
        ],
        compiler_params=PARAMS,
        cost_estimate=cost(20 * cells, 18 * cells),
        name="update",
    )(summed, sum_own, *scaled, base)
    return (
        keys[None],
        input_grads[None],
        merged[None],
        first_out[None],
        second_out[None],
        new_momentum,
        new_global,
    )


def solution(mesh):
    sharded = P("rep", "fsdp", None)
    rows = P(("fsdp", "rep"), None)
    return jax.shard_map(
        body,
        mesh=mesh,
        in_specs=(sharded,) * 6 + (rows,) * 2,
        out_specs=(sharded,) * 5 + (rows,) * 2,
        check_vma=False,
    )
```

```python
import functools

import jax
import jax.numpy as jnp
from jax import lax
from jax.experimental import pallas as pl
from jax.experimental.pallas import tpu as pltpu
from jax.sharding import PartitionSpec as P

HEAD = 128
SEQ = 1024

learning_rate = 0.002
beta_one = 0.9
beta_two = 0.95
adam_epsilon = 1e-08
weight_decay = 0.1
outer_rate = 0.7
outer_beta = 0.9
mixing = 0.5
rope_base = 500000.0

VMEM = pl.BlockSpec(memory_space=pltpu.VMEM)
ANY = pl.BlockSpec(memory_space=pl.ANY)
PARAMS = pltpu.CompilerParams(vmem_limit_bytes=10 * 1024 * 1024)
F32 = jnp.float32
BF16 = jnp.bfloat16


def array(shape, kind):
    return jax.ShapeDtypeStruct(shape, kind)


def cost(flops, bytes_accessed):
    return pl.CostEstimate(
        flops=10 * flops, bytes_accessed=10 * bytes_accessed, transcendentals=0
    )


def position(line):
    shard = lax.axis_index("fsdp")
    place, core = lax.div(shard, 2), lax.rem(shard, 2)
    ahead = 1 - 2 * core
    behind = jnp.where(core == 0, place, line - 1 - place)
    return place, core, ahead, behind


def block_at(place, parity, rows):
    return pl.multiple_of((2 * place + parity) * rows, 128)


def rotate_block(values, cosine, sines):
    heads = []
    for at in range(0, values.shape[1], HEAD):
        head = values[:, at : at + HEAD]
        heads.append(head * cosine + pltpu.roll(head, HEAD // 2, 1) * sines)
    return jnp.concatenate(heads, axis=1)


def rope_tables(shard, tokens):
    half_size = HEAD // 2
    token = lax.broadcasted_iota(jnp.int32, (tokens, HEAD), 0)
    column = lax.broadcasted_iota(jnp.int32, (tokens, HEAD), 1)
    exponents = lax.rem(column, half_size).astype(F32) * (2.0 / HEAD)
    inverse_freq = jnp.power(F32(rope_base), -exponents)
    angles = lax.rem(shard * tokens + token, SEQ).astype(F32) * inverse_freq
    sines = jnp.sin(angles)
    return jnp.cos(angles), jnp.where(column < half_size, -sines, sines)


def gradient_term(x, xp, unrotated, at, size):
    columns = pl.ds(at, size)
    left = jnp.concatenate([x[:, columns], xp[:, columns]], axis=0)
    return lax.dot_general(
        left, unrotated[...], (((0,), (0,)), ((), ())), preferred_element_type=F32
    )


def project(x, xp, unrotated, piece, total, stage, other, at, grads, sem):
    columns = pl.ds(at, piece.shape[0])
    tokens = x.shape[0]
    both = jnp.concatenate([x[:, columns], xp[:, columns]], axis=0)
    total[...] += jnp.dot(both, piece[...], preferred_element_type=F32)
    made = lax.dot_general(
        unrotated[...], piece[...], (((1,), (1,)), ((), ())), preferred_element_type=F32
    ).astype(BF16)
    stage[...] = made[:tokens, :]
    other[...] = made[tokens:, :]
    pltpu.make_async_copy(stage, grads.at[:, columns], sem).start()


def project_wait(stage, grads, at, sem):
    pltpu.make_async_copy(stage, grads.at[:, pl.ds(at, stage.shape[1])], sem).wait()


def local_kernel(line, x, xp, kg, kgp, low, *refs):
    unrotated, cosine, sines, total, other, grads, stage, sem = refs
    tokens = x.shape[0]
    place, core, _, _ = position(line)
    shard = 2 * place + core
    for half, source in enumerate((kg, kgp)):
        cosines, signed = rope_tables(jnp.bitwise_xor(shard, half), tokens)
        unrotated[half * tokens : (half + 1) * tokens, :] = rotate_block(
            source[...].astype(F32), cosines, -signed
        ).astype(BF16)
        if half == 0:
            cosine[...] = cosines
            sines[...] = signed
    total[...] = jnp.zeros_like(total)
    at = block_at(place, core, low.shape[0])
    project(x, xp, unrotated, low, total, stage, other, at, grads, sem)
    project_wait(stage, grads, at, sem)


def project_kernel(line, hop, x, xp, unrotated, total_in, grads_in, *refs):
    del grads_in
    first, second, total, other, grads, stage, sems = refs
    tokens = x.shape[0]
    rows = first.shape[0]
    place, core, ahead, behind = position(line)
    total[...] = total_in[...]

    @pl.when(behind >= hop)
    def _():
        work = [(first, core), (second, 1 - core)]
        ats = [block_at(place - hop * ahead, parity, rows) for _, parity in work]
        for i, (piece, _) in enumerate(work):
            into = other.at[:, i * rows : (i + 1) * rows]
            project(
                x, xp, unrotated, piece, total, stage.at[i], into, ats[i], grads, sems.at[i]
            )
        for i in range(2):
            project_wait(stage.at[i], grads, ats[i], sems.at[i])

    if hop == line - 1:
        other[:, 2 * rows :] = total[tokens:, :].astype(BF16)


def merge_kernel(line, cosine, sines, total, grads_in, *refs):
    del grads_in
    others = refs[:line]
    keys, grads, partial, sems, sem = refs[line:]
    tokens, _ = keys.shape
    rows = others[0].shape[1]
    place, core, ahead, behind = position(line)
    work = [(behind >= 0, place, 1 - core, others[0].at[:, :])]
    for hop in range(1, line):
        for i, parity in enumerate((1 - core, core)):
            part = others[hop].at[:, i * rows : (i + 1) * rows]
            work.append((behind + hop < line, place + hop * ahead, parity, part))

    def copy(i):
        _, owner, parity, part = work[i]
        at = pl.ds(block_at(owner, parity, rows), rows)
        return pltpu.make_async_copy(part, grads.at[:, at], sems.at[i])

    rest = pltpu.make_async_copy(others[line - 1].at[:, 2 * rows :], partial, sem)
    rest.start()
    for i in range(len(work)):
        pl.when(work[i][0])(lambda i=i: copy(i).start())
    rest.wait()
    keys[...] = rotate_block(
        total[:tokens, :] + partial[...].astype(F32), cosine[...], sines[...]
    ).astype(BF16)
    for i in range(len(work)):
        pl.when(work[i][0])(lambda i=i: copy(i).wait())


def step_kernel(line, slot, half, arrived, x, xp, unrotated, sent):
    place, core, ahead, behind = position(line)
    rows = arrived.shape[0]
    size = min(rows, 256)
    parity = core if half else 1 - core

    @pl.when(behind >= slot)
    def _():
        sent[...] = arrived[...]

    @pl.when(behind < slot)
    def _():
        owner = place + (line - slot) * ahead
        for at in range(0, rows, size):
            term = gradient_term(
                x, xp, unrotated, pl.multiple_of(block_at(owner, parity, rows) + at, 128), size
            )
            before = arrived[at : at + size, :].astype(F32)
            sent[at : at + size, :] = (term + jnp.where(behind > 0, before, 0.0)).astype(BF16)


def round_kernel(whole, low):
    low[...] = whole[...].astype(BF16)


def scale_kernel(first, second, first_scaled, second_scaled):
    first_scaled[...] = beta_one * first[...].astype(F32)
    second_scaled[...] = beta_two * second[...].astype(F32)


def split_kernel(whole, *parts):
    size = parts[0].shape[0]
    for i, part in enumerate(parts):
        part[...] = whole[i * size : (i + 1) * size, :]


def early_kernel(line, x, xp, unrotated, *refs):
    *parts, summed = refs
    place, core, _, behind = position(line)
    rows = summed.shape[0]
    size = parts[0].shape[0]
    for i, part in enumerate(parts):
        at = i * size
        term = gradient_term(
            x, xp, unrotated, pl.multiple_of(block_at(place, core, rows) + at, 128), size
        )
        other = part[...].astype(F32)
        summed[at : at + size, :] = term + jnp.where(behind < line - 1, other, 0.0)


def update_kernel(line, summed, arrived, first, second, base, merged, first_out, second_out, *scratch):
    merged_v, first_v, second_v, sem = scratch
    behind = position(line)[3]
    rows = summed.shape[0]
    parts = sem.shape[0]
    size = rows // parts
    chunk = min(size, 32)
    outs = ((merged_v, merged), (first_v, first_out), (second_v, second_out))

    def copies(part):
        at = pl.ds(part * size, size)
        return [
            pltpu.make_async_copy(source.at[at, :], target.at[at, :], sem.at[part, i])
            for i, (source, target) in enumerate(outs)
        ]

    for part in range(parts):

        def some(i, carry, part=part):
            at = pl.ds(pl.multiple_of(part * size + i * chunk, 16), chunk)
            gradient = summed[at, :] + jnp.where(behind > 0, arrived[at, :].astype(F32), 0.0)
            one = first[at, :] + (1.0 - beta_one) * gradient
            two = second[at, :] + (1.0 - beta_two) * gradient * gradient
            inverse = lax.rsqrt(two)
            step = one * (inverse * (2.0 - (two * inverse + adam_epsilon) * inverse))
            merged_v[at, :] = base[at, :] - (mixing * learning_rate) * step
            first_v[at, :] = one.astype(BF16)
            second_v[at, :] = two.astype(BF16)
            return carry

        lax.fori_loop(0, size // chunk, some, 0, unroll=True)
        for copy in copies(part):
            copy.start()
    for part in range(parts):
        for copy in copies(part):
            copy.wait()


outer_held = outer_rate * outer_beta * outer_beta
outer_slope = outer_rate * (1.0 + outer_beta)


def pack_kernel(drift, momentum, global_weights, packed):
    rows = drift.shape[0]
    packed[:rows, :] = drift[...].astype(BF16)
    packed[rows:, :] = (global_weights[...] - outer_held * momentum[...]).astype(BF16)


def repack_kernel(drift, mine, other, packed):
    rows = drift.shape[0]
    size = mine.shape[0] - rows
    packed[:rows, :] = (drift[...] + other[:rows, :].astype(F32)).astype(BF16)
    packed[rows : rows + size, :] = mine[rows:, :]
    packed[rows + size :, :] = other[rows:, :]


def outer_kernel(drift, near, far, momentum, global_weights, weights, *refs):
    base, new_momentum, new_global = refs
    rows = drift.shape[0]
    size = momentum.shape[0]
    replica = lax.axis_index("rep")
    core = lax.rem(lax.axis_index("fsdp"), 2)
    held = (None, near.at[rows:, :], far.at[rows : rows + size, :], far.at[rows + size :, :])
    for shift, other in enumerate((0, 1 + core, 2 - core, 3)):
        at = pl.ds(pl.multiple_of(jnp.bitwise_xor(replica, other) * size, size), size)
        total = drift[at, :] + near[at, :].astype(F32) + far[at, :].astype(F32)
        mean_drift = total / 4
        if shift == 0:
            moment = outer_beta * momentum[...] + mean_drift
            updated = global_weights[...] - outer_rate * (mean_drift + outer_beta * moment)
            new_momentum[...] = moment
            new_global[...] = updated
        else:
            updated = held[shift][...].astype(F32) - outer_slope * mean_drift
        base[at, :] = (mixing * (1.0 - learning_rate * weight_decay)) * weights[at, :] + (
            1.0 - mixing
        ) * updated


def pairs_of(turn, shards):
    return [
        (i * shards + j, (i ^ (1 + (j + turn) % 2)) * shards + j)
        for i in range(4)
        for j in range(shards)
    ]


def outer_pack(drift, momentum, global_weights):
    rows, columns = drift.shape
    packed = pl.pallas_call(
        pack_kernel,
        out_shape=array((rows + momentum.shape[0], columns), BF16),
        in_specs=[VMEM] * 3,
        out_specs=VMEM,
        compiler_params=PARAMS,
        cost_estimate=cost(0, 0),
        name="pack",
    )(drift, momentum, global_weights)
    near = lax.ppermute(packed, ("rep", "fsdp"), pairs_of(0, lax.axis_size("fsdp")))
    return packed, near


def outer_repack(drift, packed, near):
    rows, columns = drift.shape
    repacked = pl.pallas_call(
        repack_kernel,
        out_shape=array((2 * packed.shape[0] - rows, columns), BF16),
        in_specs=[VMEM] * 3,
        out_specs=VMEM,
        compiler_params=PARAMS,
        cost_estimate=cost(0, 0),
        name="repack",
    )(drift, packed, near)
    return repacked, lax.ppermute(repacked, ("rep", "fsdp"), pairs_of(1, lax.axis_size("fsdp")))


def outer_end(drift, near, far, momentum, global_weights, weights):
    rows, columns = drift.shape
    size = momentum.shape[0]
    return pl.pallas_call(
        outer_kernel,
        out_shape=(
            array((rows, columns), F32),
            array((size, columns), F32),
            array((size, columns), F32),
        ),
        in_specs=[VMEM] * 6,
        out_specs=(VMEM,) * 3,
        compiler_params=PARAMS,
        cost_estimate=cost(0, 0),
        name="outer",
    )(drift, near, far, momentum, global_weights, weights)


def outer_plain(drift, momentum, global_weights, weights):
    replicas = lax.axis_size("rep")
    size = momentum.shape[0]
    mean_drift = lax.psum(drift, "rep") / replicas
    whole = [lax.all_gather(a, "rep", axis=0, tiled=True) for a in (momentum, global_weights)]
    moment = outer_beta * whole[0] + mean_drift
    updated = whole[1] - outer_rate * (mean_drift + outer_beta * moment)
    base = (mixing * (1.0 - learning_rate * weight_decay)) * weights + (1.0 - mixing) * updated
    at = lax.axis_index("rep") * size
    return (
        base,
        lax.dynamic_slice_in_dim(moment, at, size, 0),
        lax.dynamic_slice_in_dim(updated, at, size, 0),
    )


def after(first, then):
    return lax.optimization_barrier((first, then))[0]


def body(inputs, key_grads, weights, first_moment, second_moment, drift, momentum, global_weights):
    x, kg, master = inputs[0], key_grads[0], weights[0]
    tokens, depth = x.shape
    rows, columns = master.shape
    shards = lax.axis_size("fsdp")
    line = shards // 2
    swap = [(i, i ^ 1) for i in range(shards)]
    onward = [(i, i + 2) for i in range(0, shards - 2, 2)] + [(shards - 2, shards - 1)]
    onward += [(i, i - 2) for i in range(3, shards, 2)] + [(1, 0)]
    piece = array((rows, columns), BF16)
    cells = rows * columns
    summed_cost = cost(4 * tokens * cells, 6 * cells + 4 * tokens * rows)

    low = master.astype(BF16)
    first_a = lax.ppermute(low, "fsdp", onward)
    master_partner = lax.ppermute(master, "fsdp", swap)
    low_partner = pl.pallas_call(
        round_kernel,
        out_shape=piece,
        in_specs=[VMEM],
        out_specs=VMEM,
        compiler_params=PARAMS,
        cost_estimate=cost(0, 0),
        name="round",
    )(after(master_partner, low))
    arrived = {1: (first_a, lax.ppermute(low_partner, "fsdp", onward))}
    xp = lax.ppermute(x, "fsdp", swap)
    kgp = lax.ppermute(kg, "fsdp", swap)

    unrotated, cosine, sines, total, other, input_grads = pl.pallas_call(
        functools.partial(local_kernel, line),
        out_shape=(
            array((2 * tokens, columns), BF16),
            array((tokens, HEAD), F32),
            array((tokens, HEAD), F32),
            array((2 * tokens, columns), F32),
            array((tokens, rows), BF16),
            array((tokens, depth), BF16),
        ),
        in_specs=[VMEM] * 5,
        out_specs=(VMEM,) * 5 + (ANY,),
        scratch_shapes=[pltpu.VMEM((tokens, rows), BF16), pltpu.SemaphoreType.DMA],
        compiler_params=PARAMS,
        cost_estimate=cost(8 * tokens * cells, 6 * cells),
        name="local",
    )(x, xp, kg, kgp, low)

    def step(slot, half, value):
        return pl.pallas_call(
            functools.partial(step_kernel, line, slot, half),
            out_shape=piece,
            in_specs=[VMEM] * 4,
            out_specs=VMEM,
            compiler_params=PARAMS,
            cost_estimate=summed_cost,
            name=f"step{slot}{'ab'[half]}",
        )(value, x, xp, unrotated)

    others = [lax.ppermute(other, "fsdp", swap)]

    def project_hop(hop, pieces, total, input_grads):
        wide = 2 * rows + (columns if hop == line - 1 else 0)
        return pl.pallas_call(
            functools.partial(project_kernel, line, hop),
            out_shape=(
                array((2 * tokens, columns), F32),
                array((tokens, wide), BF16),
                array((tokens, depth), BF16),
            ),
            in_specs=[VMEM] * 4 + [ANY] + [VMEM] * 2,
            out_specs=(VMEM, VMEM, ANY),
            scratch_shapes=[
                pltpu.VMEM((2, tokens, rows), BF16),
                pltpu.SemaphoreType.DMA((2,)),
            ],
            input_output_aliases={4: 2},
            compiler_params=PARAMS,
            cost_estimate=cost(0, 0) if hop == line - 1 else cost(16 * tokens * cells, 8 * cells),
            name=f"project{hop}",
        )(x, xp, unrotated, total, input_grads, *pieces)

    pairwise = lax.axis_size("rep") == 4
    delta = drift[0]
    if not pairwise:
        base, new_momentum, new_global = outer_plain(delta, momentum, global_weights, master)
    for slot in range(1, line):
        value = arrived[slot][0]
        if slot > 1:
            value = after(value, [sent, repacked] if pairwise and slot == 3 else sent)
        sent = step(slot, 0, value)
        first = lax.ppermute(sent, "fsdp", onward)
        value = arrived[slot][1]
        if pairwise and slot == 1:
            packed, near = outer_pack(after(delta, sent), momentum, global_weights)
        if pairwise and slot == 2:
            repacked, far = outer_repack(after(delta, sent), packed, near)
        waits = [sent, others] if slot == line - 1 else sent
        sent = step(slot, 1, after(value, waits))
        arrived[slot + 1] = (first, lax.ppermute(sent, "fsdp", onward))
        total, other, input_grads = project_hop(
            slot, arrived[slot], after(total, sent), input_grads
        )
        others.append(lax.ppermute(other, "fsdp", swap))
    sum_partner, sum_own = arrived[line]
    scaled = pl.pallas_call(
        scale_kernel,
        out_shape=(array((rows, columns), F32),) * 2,
        in_specs=[VMEM, VMEM],
        out_specs=(VMEM, VMEM),
        compiler_params=PARAMS,
        cost_estimate=cost(0, 0),
        name="scale",
    )(after(first_moment[0], sent), second_moment[0])
    sums = pl.pallas_call(
        split_kernel,
        out_shape=(array((rows // 2, columns), BF16),) * 2,
        in_specs=[VMEM],
        out_specs=(VMEM, VMEM),
        compiler_params=PARAMS,
        cost_estimate=cost(0, 0),
        name="split",
    )(after(sum_partner, [total, scaled]))
    sums_swapped = [lax.ppermute(part, "fsdp", swap) for part in sums]

    work = 2 * line - 1
    keys, input_grads = pl.pallas_call(
        functools.partial(merge_kernel, line),
        out_shape=(array((tokens, columns), BF16), array((tokens, depth), BF16)),
        in_specs=[VMEM] * 3 + [ANY] * (1 + line),
        out_specs=(VMEM, ANY),
        scratch_shapes=[
            pltpu.VMEM((tokens, columns), BF16),
            pltpu.SemaphoreType.DMA((work,)),
            pltpu.SemaphoreType.DMA,
        ],
        input_output_aliases={3: 1},
        compiler_params=PARAMS,
        cost_estimate=cost(0, 0),
        name="merge",
    )(cosine, sines, total, input_grads, *others)
    summed = pl.pallas_call(
        functools.partial(early_kernel, line),
        out_shape=array((rows, columns), F32),
        in_specs=[VMEM] * 5,
        out_specs=VMEM,
        compiler_params=PARAMS,
        cost_estimate=cost(0, 0),
        name="early",
    )(x, xp, after(unrotated, keys), *sums_swapped)
    if pairwise:
        base, new_momentum, new_global = outer_end(
            after(delta, summed), near, far, momentum, global_weights, master
        )
    sum_own = after(sum_own, base)
    update_parts = 8 if rows % 256 == 0 else 1
    merged, first_out, second_out = pl.pallas_call(
        functools.partial(update_kernel, line),
        out_shape=(
            array((rows, columns), F32),
            array((rows, columns), BF16),
            array((rows, columns), BF16),
        ),
        in_specs=[VMEM] * 5,
        out_specs=(ANY,) * 3,
        scratch_shapes=[
            pltpu.VMEM((rows, columns), F32),
            pltpu.VMEM((rows, columns), BF16),
            pltpu.VMEM((rows, columns), BF16),
            pltpu.SemaphoreType.DMA((update_parts, 3)),
        ],
        compiler_params=PARAMS,
        cost_estimate=cost(20 * cells, 18 * cells),
        name="update",
    )(summed, sum_own, *scaled, base)
    return (
        keys[None],
        input_grads[None],
        merged[None],
        first_out[None],
        second_out[None],
        new_momentum,
        new_global,
    )


def solution(mesh):
    sharded = P("rep", "fsdp", None)
    rows = P(("fsdp", "rep"), None)
    return jax.shard_map(
        body,
        mesh=mesh,
        in_specs=(sharded,) * 6 + (rows,) * 2,
        out_specs=(sharded,) * 5 + (rows,) * 2,
        check_vma=False,
    )
```

```python
import functools

import jax
import jax.numpy as jnp
from jax import lax
from jax.experimental import pallas as pl
from jax.experimental.pallas import tpu as pltpu
from jax.sharding import PartitionSpec as P

HEAD = 128
SEQ = 1024

learning_rate = 0.002
beta_one = 0.9
beta_two = 0.95
adam_epsilon = 1e-08
weight_decay = 0.1
outer_rate = 0.7
outer_beta = 0.9
mixing = 0.5
rope_base = 500000.0

VMEM = pl.BlockSpec(memory_space=pltpu.VMEM)
ANY = pl.BlockSpec(memory_space=pl.ANY)
PARAMS = pltpu.CompilerParams(vmem_limit_bytes=10 * 1024 * 1024)
F32 = jnp.float32
BF16 = jnp.bfloat16


def array(shape, kind):
    return jax.ShapeDtypeStruct(shape, kind)


def cost(flops, bytes_accessed):
    return pl.CostEstimate(
        flops=10 * flops, bytes_accessed=10 * bytes_accessed, transcendentals=0
    )


def position(line):
    shard = lax.axis_index("fsdp")
    place, core = lax.div(shard, 2), lax.rem(shard, 2)
    ahead = 1 - 2 * core
    behind = jnp.where(core == 0, place, line - 1 - place)
    return place, core, ahead, behind


def block_at(place, parity, rows):
    return pl.multiple_of((2 * place + parity) * rows, 128)


def rotate_block(values, cosine, sines):
    heads = []
    for at in range(0, values.shape[1], HEAD):
        head = values[:, at : at + HEAD]
        heads.append(head * cosine + pltpu.roll(head, HEAD // 2, 1) * sines)
    return jnp.concatenate(heads, axis=1)


def rope_tables(shard, tokens):
    half_size = HEAD // 2
    token = lax.broadcasted_iota(jnp.int32, (tokens, HEAD), 0)
    column = lax.broadcasted_iota(jnp.int32, (tokens, HEAD), 1)
    exponents = lax.rem(column, half_size).astype(F32) * (2.0 / HEAD)
    inverse_freq = jnp.power(F32(rope_base), -exponents)
    angles = lax.rem(shard * tokens + token, SEQ).astype(F32) * inverse_freq
    sines = jnp.sin(angles)
    return jnp.cos(angles), jnp.where(column < half_size, -sines, sines)


def gradient_term(x, xp, unrotated, at, size):
    columns = pl.ds(at, size)
    left = jnp.concatenate([x[:, columns], xp[:, columns]], axis=0)
    return lax.dot_general(
        left, unrotated[...], (((0,), (0,)), ((), ())), preferred_element_type=F32
    )


def project(x, xp, unrotated, piece, total, stage, other, at, grads, sem):
    columns = pl.ds(at, piece.shape[0])
    tokens = x.shape[0]
    both = jnp.concatenate([x[:, columns], xp[:, columns]], axis=0)
    total[...] += jnp.dot(both, piece[...], preferred_element_type=F32)
    made = lax.dot_general(
        unrotated[...], piece[...], (((1,), (1,)), ((), ())), preferred_element_type=F32
    ).astype(BF16)
    stage[...] = made[:tokens, :]
    other[...] = made[tokens:, :]
    pltpu.make_async_copy(stage, grads.at[:, columns], sem).start()


def project_wait(stage, grads, at, sem):
    pltpu.make_async_copy(stage, grads.at[:, pl.ds(at, stage.shape[1])], sem).wait()


def local_kernel(line, x, xp, kg, kgp, low, *refs):
    unrotated, cosine, sines, total, other, grads, stage, sem = refs
    tokens = x.shape[0]
    place, core, _, _ = position(line)
    shard = 2 * place + core
    for half, source in enumerate((kg, kgp)):
        cosines, signed = rope_tables(jnp.bitwise_xor(shard, half), tokens)
        unrotated[half * tokens : (half + 1) * tokens, :] = rotate_block(
            source[...].astype(F32), cosines, -signed
        ).astype(BF16)
        if half == 0:
            cosine[...] = cosines
            sines[...] = signed
    total[...] = jnp.zeros_like(total)
    at = block_at(place, core, low.shape[0])
    project(x, xp, unrotated, low, total, stage, other, at, grads, sem)
    project_wait(stage, grads, at, sem)


def project_kernel(line, hop, x, xp, unrotated, total_in, grads_in, *refs):
    del grads_in
    first, second, total, other, grads, stage, sems = refs
    tokens = x.shape[0]
    rows = first.shape[0]
    place, core, ahead, behind = position(line)
    total[...] = total_in[...]

    @pl.when(behind >= hop)
    def _():
        work = [(first, core), (second, 1 - core)]
        ats = [block_at(place - hop * ahead, parity, rows) for _, parity in work]
        for i, (piece, _) in enumerate(work):
            into = other.at[:, i * rows : (i + 1) * rows]
            project(
                x, xp, unrotated, piece, total, stage.at[i], into, ats[i], grads, sems.at[i]
            )
        for i in range(2):
            project_wait(stage.at[i], grads, ats[i], sems.at[i])

    if hop == line - 1:
        other[:, 2 * rows :] = total[tokens:, :].astype(BF16)


def merge_kernel(line, cosine, sines, total, grads_in, *refs):
    del grads_in
    others = refs[:line]
    keys, grads, partial, sems, sem = refs[line:]
    tokens, _ = keys.shape
    rows = others[0].shape[1]
    place, core, ahead, behind = position(line)
    work = [(behind >= 0, place, 1 - core, others[0].at[:, :])]
    for hop in range(1, line):
        for i, parity in enumerate((1 - core, core)):
            part = others[hop].at[:, i * rows : (i + 1) * rows]
            work.append((behind + hop < line, place + hop * ahead, parity, part))

    def copy(i):
        _, owner, parity, part = work[i]
        at = pl.ds(block_at(owner, parity, rows), rows)
        return pltpu.make_async_copy(part, grads.at[:, at], sems.at[i])

    rest = pltpu.make_async_copy(others[line - 1].at[:, 2 * rows :], partial, sem)
    rest.start()
    for i in range(len(work)):
        pl.when(work[i][0])(lambda i=i: copy(i).start())
    rest.wait()
    keys[...] = rotate_block(
        total[:tokens, :] + partial[...].astype(F32), cosine[...], sines[...]
    ).astype(BF16)
    for i in range(len(work)):
        pl.when(work[i][0])(lambda i=i: copy(i).wait())


def step_kernel(line, slot, half, arrived, x, xp, unrotated, sent):
    place, core, ahead, behind = position(line)
    rows = arrived.shape[0]
    size = min(rows, 256)
    parity = core if half else 1 - core

    @pl.when(behind >= slot)
    def _():
        sent[...] = arrived[...]

    @pl.when(behind < slot)
    def _():
        owner = place + (line - slot) * ahead
        for at in range(0, rows, size):
            term = gradient_term(
                x, xp, unrotated, pl.multiple_of(block_at(owner, parity, rows) + at, 128), size
            )
            before = arrived[at : at + size, :].astype(F32)
            sent[at : at + size, :] = (term + jnp.where(behind > 0, before, 0.0)).astype(BF16)


def round_kernel(whole, low):
    low[...] = whole[...].astype(BF16)


def scale_kernel(first, second, first_scaled, second_scaled):
    first_scaled[...] = beta_one * first[...].astype(F32)
    second_scaled[...] = beta_two * second[...].astype(F32)


def split_kernel(whole, *parts):
    size = parts[0].shape[0]
    for i, part in enumerate(parts):
        part[...] = whole[i * size : (i + 1) * size, :]


def early_kernel(line, x, xp, unrotated, *refs):
    *parts, summed = refs
    place, core, _, behind = position(line)
    rows = summed.shape[0]
    size = parts[0].shape[0]
    for i, part in enumerate(parts):
        at = i * size
        term = gradient_term(
            x, xp, unrotated, pl.multiple_of(block_at(place, core, rows) + at, 128), size
        )
        other = part[...].astype(F32)
        summed[at : at + size, :] = term + jnp.where(behind < line - 1, other, 0.0)


def update_kernel(line, summed, arrived, first, second, base, merged, first_out, second_out, *scratch):
    merged_v, first_v, second_v, sem = scratch
    behind = position(line)[3]
    rows = summed.shape[0]
    parts = sem.shape[0]
    size = rows // parts
    chunk = min(size, 32)
    outs = ((merged_v, merged), (first_v, first_out), (second_v, second_out))

    def copies(part):
        at = pl.ds(part * size, size)
        return [
            pltpu.make_async_copy(source.at[at, :], target.at[at, :], sem.at[part, i])
            for i, (source, target) in enumerate(outs)
        ]

    for part in range(parts):

        def some(i, carry, part=part):
            at = pl.ds(pl.multiple_of(part * size + i * chunk, 16), chunk)
            gradient = summed[at, :] + jnp.where(behind > 0, arrived[at, :].astype(F32), 0.0)
            one = first[at, :] + (1.0 - beta_one) * gradient
            two = second[at, :] + (1.0 - beta_two) * gradient * gradient
            inverse = lax.rsqrt(two)
            step = one * (inverse * (2.0 - (two * inverse + adam_epsilon) * inverse))
            merged_v[at, :] = base[at, :] - (mixing * learning_rate) * step
            first_v[at, :] = one.astype(BF16)
            second_v[at, :] = two.astype(BF16)
            return carry

        lax.fori_loop(0, size // chunk, some, 0, unroll=True)
        for copy in copies(part):
            copy.start()
    for part in range(parts):
        for copy in copies(part):
            copy.wait()


outer_held = outer_rate * outer_beta * outer_beta
outer_slope = outer_rate * (1.0 + outer_beta)


def pack_kernel(drift, momentum, global_weights, packed):
    rows = drift.shape[0]
    packed[:rows, :] = drift[...].astype(BF16)
    packed[rows:, :] = (global_weights[...] - outer_held * momentum[...]).astype(BF16)


def repack_kernel(drift, mine, other, packed):
    rows = drift.shape[0]
    size = mine.shape[0] - rows
    packed[:rows, :] = (drift[...] + other[:rows, :].astype(F32)).astype(BF16)
    packed[rows : rows + size, :] = mine[rows:, :]
    packed[rows + size :, :] = other[rows:, :]


def outer_kernel(drift, near, far, momentum, global_weights, weights, *refs):
    base, new_momentum, new_global = refs
    rows = drift.shape[0]
    size = momentum.shape[0]
    replica = lax.axis_index("rep")
    core = lax.rem(lax.axis_index("fsdp"), 2)
    held = (None, near.at[rows:, :], far.at[rows : rows + size, :], far.at[rows + size :, :])
    for shift, other in enumerate((0, 1 + core, 2 - core, 3)):
        at = pl.ds(pl.multiple_of(jnp.bitwise_xor(replica, other) * size, size), size)
        total = drift[at, :] + near[at, :].astype(F32) + far[at, :].astype(F32)
        mean_drift = total / 4
        if shift == 0:
            moment = outer_beta * momentum[...] + mean_drift
            updated = global_weights[...] - outer_rate * (mean_drift + outer_beta * moment)
            new_momentum[...] = moment
            new_global[...] = updated
        else:
            updated = held[shift][...].astype(F32) - outer_slope * mean_drift
        base[at, :] = (mixing * (1.0 - learning_rate * weight_decay)) * weights[at, :] + (
            1.0 - mixing
        ) * updated


def pairs_of(turn, shards):
    return [
        (i * shards + j, (i ^ (1 + (j + turn) % 2)) * shards + j)
        for i in range(4)
        for j in range(shards)
    ]


def outer_pack(drift, momentum, global_weights):
    rows, columns = drift.shape
    packed = pl.pallas_call(
        pack_kernel,
        out_shape=array((rows + momentum.shape[0], columns), BF16),
        in_specs=[VMEM] * 3,
        out_specs=VMEM,
        compiler_params=PARAMS,
        cost_estimate=cost(0, 0),
        name="pack",
    )(drift, momentum, global_weights)
    near = lax.ppermute(packed, ("rep", "fsdp"), pairs_of(0, lax.axis_size("fsdp")))
    return packed, near


def outer_repack(drift, packed, near):
    rows, columns = drift.shape
    repacked = pl.pallas_call(
        repack_kernel,
        out_shape=array((2 * packed.shape[0] - rows, columns), BF16),
        in_specs=[VMEM] * 3,
        out_specs=VMEM,
        compiler_params=PARAMS,
        cost_estimate=cost(0, 0),
        name="repack",
    )(drift, packed, near)
    return repacked, lax.ppermute(repacked, ("rep", "fsdp"), pairs_of(1, lax.axis_size("fsdp")))


def outer_end(drift, near, far, momentum, global_weights, weights):
    rows, columns = drift.shape
    size = momentum.shape[0]
    return pl.pallas_call(
        outer_kernel,
        out_shape=(
            array((rows, columns), F32),
            array((size, columns), F32),
            array((size, columns), F32),
        ),
        in_specs=[VMEM] * 6,
        out_specs=(VMEM,) * 3,
        compiler_params=PARAMS,
        cost_estimate=cost(0, 0),
        name="outer",
    )(drift, near, far, momentum, global_weights, weights)


def outer_plain(drift, momentum, global_weights, weights):
    replicas = lax.axis_size("rep")
    size = momentum.shape[0]
    mean_drift = lax.psum(drift, "rep") / replicas
    whole = [lax.all_gather(a, "rep", axis=0, tiled=True) for a in (momentum, global_weights)]
    moment = outer_beta * whole[0] + mean_drift
    updated = whole[1] - outer_rate * (mean_drift + outer_beta * moment)
    base = (mixing * (1.0 - learning_rate * weight_decay)) * weights + (1.0 - mixing) * updated
    at = lax.axis_index("rep") * size
    return (
        base,
        lax.dynamic_slice_in_dim(moment, at, size, 0),
        lax.dynamic_slice_in_dim(updated, at, size, 0),
    )


def after(first, then):
    return lax.optimization_barrier((first, then))[0]


def body(inputs, key_grads, weights, first_moment, second_moment, drift, momentum, global_weights):
    x, kg, master = inputs[0], key_grads[0], weights[0]
    tokens, depth = x.shape
    rows, columns = master.shape
    shards = lax.axis_size("fsdp")
    line = shards // 2
    swap = [(i, i ^ 1) for i in range(shards)]
    onward = [(i, i + 2) for i in range(0, shards - 2, 2)] + [(shards - 2, shards - 1)]
    onward += [(i, i - 2) for i in range(3, shards, 2)] + [(1, 0)]
    piece = array((rows, columns), BF16)
    cells = rows * columns
    summed_cost = cost(4 * tokens * cells, 6 * cells + 4 * tokens * rows)

    low = pl.pallas_call(
        round_kernel,
        out_shape=piece,
        in_specs=[VMEM],
        out_specs=VMEM,
        compiler_params=PARAMS,
        cost_estimate=cost(0, 0),
        name="round",
    )(master)
    first_a = lax.ppermute(low, "fsdp", onward)
    low_partner = lax.ppermute(low, "fsdp", swap)
    arrived = {1: (first_a, lax.ppermute(low_partner, "fsdp", onward))}
    xp = lax.ppermute(x, "fsdp", swap)
    kgp = lax.ppermute(kg, "fsdp", swap)

    unrotated, cosine, sines, total, other, input_grads = pl.pallas_call(
        functools.partial(local_kernel, line),
        out_shape=(
            array((2 * tokens, columns), BF16),
            array((tokens, HEAD), F32),
            array((tokens, HEAD), F32),
            array((2 * tokens, columns), F32),
            array((tokens, rows), BF16),
            array((tokens, depth), BF16),
        ),
        in_specs=[VMEM] * 5,
        out_specs=(VMEM,) * 5 + (ANY,),
        scratch_shapes=[pltpu.VMEM((tokens, rows), BF16), pltpu.SemaphoreType.DMA],
        compiler_params=PARAMS,
        cost_estimate=cost(8 * tokens * cells, 6 * cells),
        name="local",
    )(x, xp, kg, kgp, low)

    def step(slot, half, value):
        return pl.pallas_call(
            functools.partial(step_kernel, line, slot, half),
            out_shape=piece,
            in_specs=[VMEM] * 4,
            out_specs=VMEM,
            compiler_params=PARAMS,
            cost_estimate=summed_cost,
            name=f"step{slot}{'ab'[half]}",
        )(value, x, xp, unrotated)

    others = [lax.ppermute(other, "fsdp", swap)]

    def project_hop(hop, pieces, total, input_grads):
        wide = 2 * rows + (columns if hop == line - 1 else 0)
        return pl.pallas_call(
            functools.partial(project_kernel, line, hop),
            out_shape=(
                array((2 * tokens, columns), F32),
                array((tokens, wide), BF16),
                array((tokens, depth), BF16),
            ),
            in_specs=[VMEM] * 4 + [ANY] + [VMEM] * 2,
            out_specs=(VMEM, VMEM, ANY),
            scratch_shapes=[
                pltpu.VMEM((2, tokens, rows), BF16),
                pltpu.SemaphoreType.DMA((2,)),
            ],
            input_output_aliases={4: 2},
            compiler_params=PARAMS,
            cost_estimate=cost(0, 0) if hop == line - 1 else cost(16 * tokens * cells, 8 * cells),
            name=f"project{hop}",
        )(x, xp, unrotated, total, input_grads, *pieces)

    pairwise = lax.axis_size("rep") == 4
    delta = drift[0]
    if not pairwise:
        base, new_momentum, new_global = outer_plain(delta, momentum, global_weights, master)
    for slot in range(1, line):
        value = arrived[slot][0]
        if slot > 1:
            value = after(value, [sent, repacked] if pairwise and slot == 3 else sent)
        sent = step(slot, 0, value)
        first = lax.ppermute(sent, "fsdp", onward)
        value = arrived[slot][1]
        if pairwise and slot == 1:
            packed, near = outer_pack(after(delta, sent), momentum, global_weights)
        if pairwise and slot == 2:
            repacked, far = outer_repack(after(delta, sent), packed, near)
        waits = [sent, others] if slot == line - 1 else sent
        sent = step(slot, 1, after(value, waits))
        arrived[slot + 1] = (first, lax.ppermute(sent, "fsdp", onward))
        total, other, input_grads = project_hop(
            slot, arrived[slot], after(total, sent), input_grads
        )
        others.append(lax.ppermute(other, "fsdp", swap))
    sum_partner, sum_own = arrived[line]
    scaled = pl.pallas_call(
        scale_kernel,
        out_shape=(array((rows, columns), F32),) * 2,
        in_specs=[VMEM, VMEM],
        out_specs=(VMEM, VMEM),
        compiler_params=PARAMS,
        cost_estimate=cost(0, 0),
        name="scale",
    )(after(first_moment[0], sent), second_moment[0])
    sums = pl.pallas_call(
        split_kernel,
        out_shape=(array((rows // 2, columns), BF16),) * 2,
        in_specs=[VMEM],
        out_specs=(VMEM, VMEM),
        compiler_params=PARAMS,
        cost_estimate=cost(0, 0),
        name="split",
    )(after(sum_partner, [total, scaled]))
    sums_swapped = [lax.ppermute(part, "fsdp", swap) for part in sums]

    work = 2 * line - 1
    keys, input_grads = pl.pallas_call(
        functools.partial(merge_kernel, line),
        out_shape=(array((tokens, columns), BF16), array((tokens, depth), BF16)),
        in_specs=[VMEM] * 3 + [ANY] * (1 + line),
        out_specs=(VMEM, ANY),
        scratch_shapes=[
            pltpu.VMEM((tokens, columns), BF16),
            pltpu.SemaphoreType.DMA((work,)),
            pltpu.SemaphoreType.DMA,
        ],
        input_output_aliases={3: 1},
        compiler_params=PARAMS,
        cost_estimate=cost(0, 0),
        name="merge",
    )(cosine, sines, total, input_grads, *others)
    summed = pl.pallas_call(
        functools.partial(early_kernel, line),
        out_shape=array((rows, columns), F32),
        in_specs=[VMEM] * 5,
        out_specs=VMEM,
        compiler_params=PARAMS,
        cost_estimate=cost(0, 0),
        name="early",
    )(x, xp, after(unrotated, keys), *sums_swapped)
    if pairwise:
        base, new_momentum, new_global = outer_end(
            after(delta, summed), near, far, momentum, global_weights, master
        )
    sum_own = after(sum_own, base)
    update_parts = 8 if rows % 256 == 0 else 1
    merged, first_out, second_out = pl.pallas_call(
        functools.partial(update_kernel, line),
        out_shape=(
            array((rows, columns), F32),
            array((rows, columns), BF16),
            array((rows, columns), BF16),
        ),
        in_specs=[VMEM] * 5,
        out_specs=(ANY,) * 3,
        scratch_shapes=[
            pltpu.VMEM((rows, columns), F32),
            pltpu.VMEM((rows, columns), BF16),
            pltpu.VMEM((rows, columns), BF16),
            pltpu.SemaphoreType.DMA((update_parts, 3)),
        ],
        compiler_params=PARAMS,
        cost_estimate=cost(20 * cells, 18 * cells),
        name="update",
    )(summed, sum_own, *scaled, base)
    return (
        keys[None],
        input_grads[None],
        merged[None],
        first_out[None],
        second_out[None],
        new_momentum,
        new_global,
    )


def solution(mesh):
    sharded = P("rep", "fsdp", None)
    rows = P(("fsdp", "rep"), None)
    return jax.shard_map(
        body,
        mesh=mesh,
        in_specs=(sharded,) * 6 + (rows,) * 2,
        out_specs=(sharded,) * 5 + (rows,) * 2,
        check_vma=False,
    )
```

```python
import functools

import jax
import jax.numpy as jnp
from jax import lax
from jax.experimental import pallas as pl
from jax.experimental.pallas import tpu as pltpu
from jax.sharding import PartitionSpec as P

HEAD = 128
SEQ = 1024

learning_rate = 0.002
beta_one = 0.9
beta_two = 0.95
adam_epsilon = 1e-08
weight_decay = 0.1
outer_rate = 0.7
outer_beta = 0.9
mixing = 0.5
rope_base = 500000.0

VMEM = pl.BlockSpec(memory_space=pltpu.VMEM)
ANY = pl.BlockSpec(memory_space=pl.ANY)
PARAMS = pltpu.CompilerParams(vmem_limit_bytes=10 * 1024 * 1024)
F32 = jnp.float32
BF16 = jnp.bfloat16


def array(shape, kind):
    return jax.ShapeDtypeStruct(shape, kind)


def cost(flops, bytes_accessed):
    return pl.CostEstimate(
        flops=10 * flops, bytes_accessed=10 * bytes_accessed, transcendentals=0
    )


def position(line):
    shard = lax.axis_index("fsdp")
    place, core = lax.div(shard, 2), lax.rem(shard, 2)
    ahead = 1 - 2 * core
    behind = jnp.where(core == 0, place, line - 1 - place)
    return place, core, ahead, behind


def block_at(place, parity, rows):
    return pl.multiple_of((2 * place + parity) * rows, 128)


def rotate_block(values, cosine, sines):
    heads = []
    for at in range(0, values.shape[1], HEAD):
        head = values[:, at : at + HEAD]
        heads.append(head * cosine + pltpu.roll(head, HEAD // 2, 1) * sines)
    return jnp.concatenate(heads, axis=1)


def rope_tables(shard, tokens):
    half_size = HEAD // 2
    token = lax.broadcasted_iota(jnp.int32, (tokens, HEAD), 0)
    column = lax.broadcasted_iota(jnp.int32, (tokens, HEAD), 1)
    exponents = lax.rem(column, half_size).astype(F32) * (2.0 / HEAD)
    inverse_freq = jnp.power(F32(rope_base), -exponents)
    angles = lax.rem(shard * tokens + token, SEQ).astype(F32) * inverse_freq
    sines = jnp.sin(angles)
    return jnp.cos(angles), jnp.where(column < half_size, -sines, sines)


def gradient_term(x, xp, unrotated, at, size):
    columns = pl.ds(at, size)
    left = jnp.concatenate([x[:, columns], xp[:, columns]], axis=0)
    return lax.dot_general(
        left, unrotated[...], (((0,), (0,)), ((), ())), preferred_element_type=F32
    )


def project(x, xp, unrotated, piece, total, stage, other, at, grads, sem):
    columns = pl.ds(at, piece.shape[0])
    tokens = x.shape[0]
    both = jnp.concatenate([x[:, columns], xp[:, columns]], axis=0)
    total[...] += jnp.dot(both, piece[...], preferred_element_type=F32)
    made = lax.dot_general(
        unrotated[...], piece[...], (((1,), (1,)), ((), ())), preferred_element_type=F32
    ).astype(BF16)
    stage[...] = made[:tokens, :]
    other[...] = made[tokens:, :]
    pltpu.make_async_copy(stage, grads.at[:, columns], sem).start()


def project_wait(stage, grads, at, sem):
    pltpu.make_async_copy(stage, grads.at[:, pl.ds(at, stage.shape[1])], sem).wait()


def local_kernel(line, x, xp, kg, kgp, low, *refs):
    unrotated, cosine, sines, total, other, grads, stage, sem = refs
    tokens = x.shape[0]
    place, core, _, _ = position(line)
    shard = 2 * place + core
    for half, source in enumerate((kg, kgp)):
        cosines, signed = rope_tables(jnp.bitwise_xor(shard, half), tokens)
        unrotated[half * tokens : (half + 1) * tokens, :] = rotate_block(
            source[...].astype(F32), cosines, -signed
        ).astype(BF16)
        if half == 0:
            cosine[...] = cosines
            sines[...] = signed
    total[...] = jnp.zeros_like(total)
    at = block_at(place, core, low.shape[0])
    project(x, xp, unrotated, low, total, stage, other, at, grads, sem)
    project_wait(stage, grads, at, sem)


def project_kernel(line, hop, x, xp, unrotated, total_in, grads_in, *refs):
    del grads_in
    first, second, total, other, grads, stage, sems = refs
    tokens = x.shape[0]
    rows = first.shape[0]
    place, core, ahead, behind = position(line)
    total[...] = total_in[...]

    @pl.when(behind >= hop)
    def _():
        work = [(first, core), (second, 1 - core)]
        ats = [block_at(place - hop * ahead, parity, rows) for _, parity in work]
        for i, (piece, _) in enumerate(work):
            into = other.at[:, i * rows : (i + 1) * rows]
            project(
                x, xp, unrotated, piece, total, stage.at[i], into, ats[i], grads, sems.at[i]
            )
        for i in range(2):
            project_wait(stage.at[i], grads, ats[i], sems.at[i])

    if hop == line - 1:
        other[:, 2 * rows :] = total[tokens:, :].astype(BF16)


def merge_kernel(line, cosine, sines, total, grads_in, *refs):
    del grads_in
    others = refs[:line]
    keys, grads, partial, sems, sem = refs[line:]
    tokens, _ = keys.shape
    rows = others[0].shape[1]
    place, core, ahead, behind = position(line)
    work = [(behind >= 0, place, 1 - core, others[0].at[:, :])]
    for hop in range(1, line):
        for i, parity in enumerate((1 - core, core)):
            part = others[hop].at[:, i * rows : (i + 1) * rows]
            work.append((behind + hop < line, place + hop * ahead, parity, part))

    def copy(i):
        _, owner, parity, part = work[i]
        at = pl.ds(block_at(owner, parity, rows), rows)
        return pltpu.make_async_copy(part, grads.at[:, at], sems.at[i])

    rest = pltpu.make_async_copy(others[line - 1].at[:, 2 * rows :], partial, sem)
    rest.start()
    for i in range(len(work)):
        pl.when(work[i][0])(lambda i=i: copy(i).start())
    rest.wait()
    keys[...] = rotate_block(
        total[:tokens, :] + partial[...].astype(F32), cosine[...], sines[...]
    ).astype(BF16)
    for i in range(len(work)):
        pl.when(work[i][0])(lambda i=i: copy(i).wait())


def step_kernel(line, slot, half, arrived, x, xp, unrotated, sent):
    place, core, ahead, behind = position(line)
    rows = arrived.shape[0]
    size = min(rows, 256)
    parity = core if half else 1 - core

    @pl.when(behind >= slot)
    def _():
        sent[...] = arrived[...]

    @pl.when(behind < slot)
    def _():
        owner = place + (line - slot) * ahead
        for at in range(0, rows, size):
            term = gradient_term(
                x, xp, unrotated, pl.multiple_of(block_at(owner, parity, rows) + at, 128), size
            )
            before = arrived[at : at + size, :].astype(F32)
            sent[at : at + size, :] = (term + jnp.where(behind > 0, before, 0.0)).astype(BF16)


def round_kernel(whole, low):
    low[...] = whole[...].astype(BF16)


def scale_kernel(first, second, first_scaled, second_scaled):
    first_scaled[...] = beta_one * first[...].astype(F32)
    second_scaled[...] = beta_two * second[...].astype(F32)


def split_kernel(whole, *parts):
    size = parts[0].shape[0]
    for i, part in enumerate(parts):
        part[...] = whole[i * size : (i + 1) * size, :]


def early_kernel(line, x, xp, unrotated, *refs):
    *parts, summed = refs
    place, core, _, behind = position(line)
    rows = summed.shape[0]
    size = parts[0].shape[0]
    for i, part in enumerate(parts):
        at = i * size
        term = gradient_term(
            x, xp, unrotated, pl.multiple_of(block_at(place, core, rows) + at, 128), size
        )
        other = part[...].astype(F32)
        summed[at : at + size, :] = term + jnp.where(behind < line - 1, other, 0.0)


def update_kernel(line, summed, arrived, first, second, base, merged, first_out, second_out, *scratch):
    merged_v, first_v, second_v, sem = scratch
    behind = position(line)[3]
    rows = summed.shape[0]
    parts = sem.shape[0]
    size = rows // parts
    chunk = min(size, 32)
    outs = ((merged_v, merged), (first_v, first_out), (second_v, second_out))

    def copies(part):
        at = pl.ds(part * size, size)
        return [
            pltpu.make_async_copy(source.at[at, :], target.at[at, :], sem.at[part, i])
            for i, (source, target) in enumerate(outs)
        ]

    for part in range(parts):

        def some(i, carry, part=part):
            at = pl.ds(pl.multiple_of(part * size + i * chunk, 16), chunk)
            gradient = summed[at, :] + jnp.where(behind > 0, arrived[at, :].astype(F32), 0.0)
            one = first[at, :] + (1.0 - beta_one) * gradient
            two = second[at, :] + (1.0 - beta_two) * gradient * gradient
            inverse = lax.rsqrt(two)
            step = one * (inverse * (2.0 - (two * inverse + adam_epsilon) * inverse))
            merged_v[at, :] = base[at, :] - (mixing * learning_rate) * step
            first_v[at, :] = one.astype(BF16)
            second_v[at, :] = two.astype(BF16)
            return carry

        lax.fori_loop(0, size // chunk, some, 0, unroll=True)
        for copy in copies(part):
            copy.start()
    for part in range(parts):
        for copy in copies(part):
            copy.wait()


outer_held = outer_rate * outer_beta * outer_beta
outer_slope = outer_rate * (1.0 + outer_beta)


def pack_kernel(drift, momentum, global_weights, packed):
    rows = drift.shape[0]
    packed[:rows, :] = drift[...].astype(BF16)
    packed[rows:, :] = (global_weights[...] - outer_held * momentum[...]).astype(BF16)


def repack_kernel(drift, mine, other, packed):
    rows = drift.shape[0]
    size = mine.shape[0] - rows
    packed[:rows, :] = (drift[...] + other[:rows, :].astype(F32)).astype(BF16)
    packed[rows : rows + size, :] = mine[rows:, :]
    packed[rows + size :, :] = other[rows:, :]


def outer_kernel(drift, near, far, momentum, global_weights, weights, *refs):
    base, new_momentum, new_global = refs
    rows = drift.shape[0]
    size = momentum.shape[0]
    replica = lax.axis_index("rep")
    core = lax.rem(lax.axis_index("fsdp"), 2)
    held = (None, near.at[rows:, :], far.at[rows : rows + size, :], far.at[rows + size :, :])
    for shift, other in enumerate((0, 1 + core, 2 - core, 3)):
        at = pl.ds(pl.multiple_of(jnp.bitwise_xor(replica, other) * size, size), size)
        total = drift[at, :] + near[at, :].astype(F32) + far[at, :].astype(F32)
        mean_drift = total / 4
        if shift == 0:
            moment = outer_beta * momentum[...] + mean_drift
            updated = global_weights[...] - outer_rate * (mean_drift + outer_beta * moment)
            new_momentum[...] = moment
            new_global[...] = updated
        else:
            updated = held[shift][...].astype(F32) - outer_slope * mean_drift
        base[at, :] = (mixing * (1.0 - learning_rate * weight_decay)) * weights[at, :] + (
            1.0 - mixing
        ) * updated


def pairs_of(turn, shards):
    return [
        (i * shards + j, (i ^ (1 + (j + turn) % 2)) * shards + j)
        for i in range(4)
        for j in range(shards)
    ]


def outer_pack(drift, momentum, global_weights):
    rows, columns = drift.shape
    packed = pl.pallas_call(
        pack_kernel,
        out_shape=array((rows + momentum.shape[0], columns), BF16),
        in_specs=[VMEM] * 3,
        out_specs=VMEM,
        compiler_params=PARAMS,
        cost_estimate=cost(0, 0),
        name="pack",
    )(drift, momentum, global_weights)
    near = lax.ppermute(packed, ("rep", "fsdp"), pairs_of(0, lax.axis_size("fsdp")))
    return packed, near


def outer_repack(drift, packed, near):
    rows, columns = drift.shape
    repacked = pl.pallas_call(
        repack_kernel,
        out_shape=array((2 * packed.shape[0] - rows, columns), BF16),
        in_specs=[VMEM] * 3,
        out_specs=VMEM,
        compiler_params=PARAMS,
        cost_estimate=cost(0, 0),
        name="repack",
    )(drift, packed, near)
    return repacked, lax.ppermute(repacked, ("rep", "fsdp"), pairs_of(1, lax.axis_size("fsdp")))


def outer_end(drift, near, far, momentum, global_weights, weights):
    rows, columns = drift.shape
    size = momentum.shape[0]
    return pl.pallas_call(
        outer_kernel,
        out_shape=(
            array((rows, columns), F32),
            array((size, columns), F32),
            array((size, columns), F32),
        ),
        in_specs=[VMEM] * 6,
        out_specs=(VMEM,) * 3,
        compiler_params=PARAMS,
        cost_estimate=cost(0, 0),
        name="outer",
    )(drift, near, far, momentum, global_weights, weights)


def outer_plain(drift, momentum, global_weights, weights):
    replicas = lax.axis_size("rep")
    size = momentum.shape[0]
    mean_drift = lax.psum(drift, "rep") / replicas
    whole = [lax.all_gather(a, "rep", axis=0, tiled=True) for a in (momentum, global_weights)]
    moment = outer_beta * whole[0] + mean_drift
    updated = whole[1] - outer_rate * (mean_drift + outer_beta * moment)
    base = (mixing * (1.0 - learning_rate * weight_decay)) * weights + (1.0 - mixing) * updated
    at = lax.axis_index("rep") * size
    return (
        base,
        lax.dynamic_slice_in_dim(moment, at, size, 0),
        lax.dynamic_slice_in_dim(updated, at, size, 0),
    )


def after(first, then):
    return lax.optimization_barrier((first, then))[0]


def body(inputs, key_grads, weights, first_moment, second_moment, drift, momentum, global_weights):
    x, kg, master = inputs[0], key_grads[0], weights[0]
    tokens, depth = x.shape
    rows, columns = master.shape
    shards = lax.axis_size("fsdp")
    line = shards // 2
    swap = [(i, i ^ 1) for i in range(shards)]
    onward = [(i, i + 2) for i in range(0, shards - 2, 2)] + [(shards - 2, shards - 1)]
    onward += [(i, i - 2) for i in range(3, shards, 2)] + [(1, 0)]
    piece = array((rows, columns), BF16)
    cells = rows * columns
    summed_cost = cost(4 * tokens * cells, 6 * cells + 4 * tokens * rows)

    low = pl.pallas_call(
        round_kernel,
        out_shape=piece,
        grid=(4,),
        in_specs=[pl.BlockSpec((rows // 4, columns), lambda i: (i, 0))],
        out_specs=pl.BlockSpec((rows // 4, columns), lambda i: (i, 0)),
        compiler_params=PARAMS,
        cost_estimate=cost(0, 0),
        name="round",
    )(master)
    first_a = lax.ppermute(low, "fsdp", onward)
    low_partner = lax.ppermute(low, "fsdp", swap)
    arrived = {1: (first_a, lax.ppermute(low_partner, "fsdp", onward))}
    xp = lax.ppermute(x, "fsdp", swap)
    kgp = lax.ppermute(kg, "fsdp", swap)

    unrotated, cosine, sines, total, other, input_grads = pl.pallas_call(
        functools.partial(local_kernel, line),
        out_shape=(
            array((2 * tokens, columns), BF16),
            array((tokens, HEAD), F32),
            array((tokens, HEAD), F32),
            array((2 * tokens, columns), F32),
            array((tokens, rows), BF16),
            array((tokens, depth), BF16),
        ),
        in_specs=[VMEM] * 5,
        out_specs=(VMEM,) * 5 + (ANY,),
        scratch_shapes=[pltpu.VMEM((tokens, rows), BF16), pltpu.SemaphoreType.DMA],
        compiler_params=PARAMS,
        cost_estimate=cost(8 * tokens * cells, 6 * cells),
        name="local",
    )(x, xp, kg, kgp, low)

    def step(slot, half, value):
        return pl.pallas_call(
            functools.partial(step_kernel, line, slot, half),
            out_shape=piece,
            in_specs=[VMEM] * 4,
            out_specs=VMEM,
            compiler_params=PARAMS,
            cost_estimate=summed_cost,
            name=f"step{slot}{'ab'[half]}",
        )(value, x, xp, unrotated)

    others = [lax.ppermute(other, "fsdp", swap)]

    def project_hop(hop, pieces, total, input_grads):
        wide = 2 * rows + (columns if hop == line - 1 else 0)
        return pl.pallas_call(
            functools.partial(project_kernel, line, hop),
            out_shape=(
                array((2 * tokens, columns), F32),
                array((tokens, wide), BF16),
                array((tokens, depth), BF16),
            ),
            in_specs=[VMEM] * 4 + [ANY] + [VMEM] * 2,
            out_specs=(VMEM, VMEM, ANY),
            scratch_shapes=[
                pltpu.VMEM((2, tokens, rows), BF16),
                pltpu.SemaphoreType.DMA((2,)),
            ],
            input_output_aliases={4: 2},
            compiler_params=PARAMS,
            cost_estimate=cost(0, 0) if hop == line - 1 else cost(16 * tokens * cells, 8 * cells),
            name=f"project{hop}",
        )(x, xp, unrotated, total, input_grads, *pieces)

    pairwise = lax.axis_size("rep") == 4
    delta = drift[0]
    if not pairwise:
        base, new_momentum, new_global = outer_plain(delta, momentum, global_weights, master)
    for slot in range(1, line):
        value = arrived[slot][0]
        if slot > 1:
            value = after(value, [sent, repacked] if pairwise and slot == 3 else sent)
        sent = step(slot, 0, value)
        first = lax.ppermute(sent, "fsdp", onward)
        value = arrived[slot][1]
        if pairwise and slot == 1:
            packed, near = outer_pack(after(delta, sent), momentum, global_weights)
        if pairwise and slot == 2:
            repacked, far = outer_repack(after(delta, sent), packed, near)
        waits = [sent, others] if slot == line - 1 else sent
        sent = step(slot, 1, after(value, waits))
        arrived[slot + 1] = (first, lax.ppermute(sent, "fsdp", onward))
        total, other, input_grads = project_hop(
            slot, arrived[slot], after(total, sent), input_grads
        )
        others.append(lax.ppermute(other, "fsdp", swap))
    sum_partner, sum_own = arrived[line]
    scaled = pl.pallas_call(
        scale_kernel,
        out_shape=(array((rows, columns), F32),) * 2,
        in_specs=[VMEM, VMEM],
        out_specs=(VMEM, VMEM),
        compiler_params=PARAMS,
        cost_estimate=cost(0, 0),
        name="scale",
    )(after(first_moment[0], sent), second_moment[0])
    sums = pl.pallas_call(
        split_kernel,
        out_shape=(array((rows // 2, columns), BF16),) * 2,
        in_specs=[VMEM],
        out_specs=(VMEM, VMEM),
        compiler_params=PARAMS,
        cost_estimate=cost(0, 0),
        name="split",
    )(after(sum_partner, [total, scaled]))
    sums_swapped = [lax.ppermute(part, "fsdp", swap) for part in sums]

    work = 2 * line - 1
    keys, input_grads = pl.pallas_call(
        functools.partial(merge_kernel, line),
        out_shape=(array((tokens, columns), BF16), array((tokens, depth), BF16)),
        in_specs=[VMEM] * 3 + [ANY] * (1 + line),
        out_specs=(VMEM, ANY),
        scratch_shapes=[
            pltpu.VMEM((tokens, columns), BF16),
            pltpu.SemaphoreType.DMA((work,)),
            pltpu.SemaphoreType.DMA,
        ],
        input_output_aliases={3: 1},
        compiler_params=PARAMS,
        cost_estimate=cost(0, 0),
        name="merge",
    )(cosine, sines, total, input_grads, *others)
    summed = pl.pallas_call(
        functools.partial(early_kernel, line),
        out_shape=array((rows, columns), F32),
        in_specs=[VMEM] * 5,
        out_specs=VMEM,
        compiler_params=PARAMS,
        cost_estimate=cost(0, 0),
        name="early",
    )(x, xp, after(unrotated, keys), *sums_swapped)
    if pairwise:
        base, new_momentum, new_global = outer_end(
            after(delta, summed), near, far, momentum, global_weights, master
        )
    sum_own = after(sum_own, base)
    update_parts = 8 if rows % 256 == 0 else 1
    merged, first_out, second_out = pl.pallas_call(
        functools.partial(update_kernel, line),
        out_shape=(
            array((rows, columns), F32),
            array((rows, columns), BF16),
            array((rows, columns), BF16),
        ),
        in_specs=[VMEM] * 5,
        out_specs=(ANY,) * 3,
        scratch_shapes=[
            pltpu.VMEM((rows, columns), F32),
            pltpu.VMEM((rows, columns), BF16),
            pltpu.VMEM((rows, columns), BF16),
            pltpu.SemaphoreType.DMA((update_parts, 3)),
        ],
        compiler_params=PARAMS,
        cost_estimate=cost(20 * cells, 18 * cells),
        name="update",
    )(summed, sum_own, *scaled, base)
    return (
        keys[None],
        input_grads[None],
        merged[None],
        first_out[None],
        second_out[None],
        new_momentum,
        new_global,
    )


def solution(mesh):
    sharded = P("rep", "fsdp", None)
    rows = P(("fsdp", "rep"), None)
    return jax.shard_map(
        body,
        mesh=mesh,
        in_specs=(sharded,) * 6 + (rows,) * 2,
        out_specs=(sharded,) * 5 + (rows,) * 2,
        check_vma=False,
    )
```
